128 devices in a mesh: leaf: 128 (over x, z, y, core).
Axes of the slice: x: 4, y: 4, z: 4, core: 2. Of those that a mesh axis runs over, the one named last changes fastest.
Arguments:
- points: bfloat16 [64, 524288], P(None, 'leaf'), may hold values from -6 to 6
- coords: float32 [3, 524288], P(None, 'leaf'), may hold values from 0 to 9
- leaf_order: int32 [524288], P('leaf'), may hold values from 0 to 524287, as said below
- leaf_basis: bfloat16 [2048, 64, 256], P('leaf'), may hold values from -0.375 to 0.375
- transfer: bfloat16 [2048, 64, 64], P('leaf'), may hold values from -0.25 to 0.25
- far_coupling: bfloat16 [16384, 64, 64], P('leaf'), may hold values from -0.75 to 0.75
- far_target: int32 [16384], P('leaf'), may hold values from 0 to 15
- far_source: int32 [16384], P('leaf'), may hold values from 0 to 2047, as said below
- far_live: int32 [16384], P('leaf'), may hold values 0 or 1
- top_coupling: bfloat16 [4096, 64, 64], P('leaf'), may hold values from -0.75 to 0.75
- top_target: int32 [4096], P('leaf'), may hold values from 0 to 1
- top_source: int32 [4096], P('leaf'), may hold values from 0 to 255, as said below
- top_live: int32 [4096], P('leaf'), may hold values 0 or 1
- near_source: int32 [2048, 12], P('leaf'), may hold values from 0 to 2047, as said below
- near_count: int32 [2048], P('leaf'), may hold values from 2 to 12, as said below
Outputs:
- product: bfloat16 [64, 524288], P(None, 'leaf')
The draws below stay inside these ranges and needn't reach their ends.
Inputs may be any that keep to these rules, and one draw needn't show every extreme that they name: `leaf_order`: within each block of 4096 positions, a permutation of the input indices of that same block. `far_source`: among the 128 slots of one device, at most 2 name leaves of any one device, and in each device's slots some device is named exactly 2 times. `top_source`: among the 32 slots of one device, at most 2 name parents of any one device, and in each device's slots some device is named exactly 2 times. near_source[t, 0] = t, and every entry of row t lies within 4 of t. `near_count`: some leaf has 12.
All inputs are finite; a program needn't handle non-finite values. No bound on the sum of `far_live` or of `top_live` on one device may be relied on, other than what follows from the above.
Results may differ from the reference program's by a relative error of at most 0.0045.
The reference program's roundings to bfloat16 on the way count: a program that leaves them out, or rounds other values in their place, can miss the bound.
Values may be sent and summed in bfloat16 or wider, within the bound.
No kernel may reach another device: no remote copies, remote signals or barrier semaphores. Data moves between devices by JAX's collectives and lax.ppermute only.
A program may use at most 64 MiB of HBM per device.

```python
import jax
import jax.numpy as jnp
from jax import lax

R = 64
K = 64
LEAF = 256
NEAR = 12
LD = 16
PD = 2
HW = 4
CL = 128
CP = 32
CAP = 2
CAPT = 2
PTS_DEV = 4096
LEAVES = 2048
PARENTS = 256
POINTS = 524288
N_LEAF = 128


def tree_order(key):
    device_count = LEAVES // LD
    key_list = jax.random.split(key, device_count)
    return jax.vmap(lambda subkey: jax.random.permutation(subkey, PTS_DEV))(key_list).astype(jnp.int32)


def draw_leaf_order(key, part):
    permuted = tree_order(key)
    device_count = permuted.shape[0]
    offsets = (jnp.arange(device_count, dtype=jnp.int32) * PTS_DEV)[:, None]
    return (permuted + offsets).reshape(-1)


def draw_coords(key, part):
    permuted = tree_order(key)
    key = jax.random.fold_in(key, 11)
    device_count = permuted.shape[0]
    inverse = jnp.argsort(permuted, axis=1).astype(jnp.int32)
    position = inverse + (jnp.arange(device_count, dtype=jnp.int32) * PTS_DEV)[:, None]
    leaf_index = (position // LEAF).reshape(-1)
    centre = 0.25 * jnp.stack([leaf_index // 64, leaf_index // 8 % 8, leaf_index % 8]).astype(jnp.float32)
    offset = jax.random.uniform(key, (3, POINTS), jnp.float32)
    return centre + offset


def pick_sources(key, per_dev, cap_size, clusters):
    device_count = LEAVES // LD

    def per_device(subkey):
        key_first, key_scores, key_shuffle, key_local = jax.random.split(subkey, 4)
        first_peer = jax.random.randint(key_first, (), 0, device_count)
        pair_index = jnp.arange(device_count * cap_size, dtype=jnp.int32)
        scores = jax.random.permutation(key_scores, device_count * cap_size).astype(jnp.int32)
        scores = jnp.where(pair_index // cap_size == first_peer, pair_index % cap_size - cap_size, scores)
        chosen = jnp.argsort(scores, stable=True)[:per_dev].astype(jnp.int32)
        owner_dev = jax.random.permutation(key_shuffle, chosen // cap_size)
        local_ids = jax.random.randint(key_local, (per_dev,), 0, clusters)
        return (owner_dev * clusters + local_ids).astype(jnp.int32)
    return jax.vmap(per_device)(jax.random.split(key, device_count)).reshape(-1)


def draw_far_source(key, part):
    key = jax.random.fold_in(key, 3)
    return pick_sources(key, CL, CAP, LD)


def draw_top_source(key, part):
    key = jax.random.fold_in(key, 5)
    return pick_sources(key, CP, CAPT, PD)


def draw_near_source(key, part):
    key = jax.random.fold_in(key, 7)
    leaf_index = jnp.arange(LEAVES, dtype=jnp.int32)[:, None]
    lowest = jnp.maximum(-HW, -leaf_index)
    highest = jnp.minimum(HW, LEAVES - 1 - leaf_index) + 1
    offset = jax.random.randint(key, (LEAVES, NEAR), lowest, highest)
    edge_offset = jnp.where(leaf_index >= HW, -HW, HW)
    slot_index = jnp.arange(NEAR, dtype=jnp.int32)[None, :]
    offset = jnp.where(slot_index == 0, 0, jnp.where(slot_index == 1, edge_offset, offset))
    return (leaf_index + offset).astype(jnp.int32)


def draw_near_count(key, part):
    key = jax.random.fold_in(key, 9)
    key_count, key_full = jax.random.split(key)
    counts = jax.random.randint(key_count, (LEAVES,), 2, NEAR + 1)
    full_leaf = jax.random.randint(key_full, (), 0, LEAVES)
    return jnp.where(jnp.arange(LEAVES, dtype=jnp.int32) == full_leaf, NEAR, counts).astype(jnp.int32)


def place_ends(array, own_key, low, high):
    place = [jax.random.randint(jax.random.fold_in(own_key, axis), (), 0, length) for axis, length in enumerate(array.shape)]
    widest = array.shape.index(max(array.shape))
    beside = place[:widest] + [(place[widest] + 1) % array.shape[widest]] + place[widest + 1:]
    return array.at[tuple(place)].set(low).at[tuple(beside)].set(high)


def level_of(key, extent, cuts, least, high):
    level = 1.0
    for axis_at, parts in cuts:
        heights = jax.random.uniform(jax.random.fold_in(jax.random.fold_in(key, 6), axis_at), (parts,), jnp.float32, least / len(cuts), high / len(cuts))
        level = level * jnp.repeat(jnp.exp(heights), extent[axis_at] // parts).reshape((-1,) + (1,) * (len(extent) - 1 - axis_at))
    return level


def scatter_about(own_key, shape, spread, reach, cuts=(), held_as=jnp.bfloat16):
    values = jax.random.normal(own_key, shape, jnp.float32) * spread
    if len(cuts) > 0:
        values = level_of(own_key, shape, cuts, -0.22, 0.18) * values
    return jnp.clip(values, min=-reach, max=reach).astype(held_as)


def setup_inputs(seed: int = 0) -> dict:
    splits = jax.random.split(jax.random.key(seed), 16)
    return {
        "points": scatter_about(splits[0], (R, POINTS), 1.0, 6.0, ((1, 128),)),
        "coords": draw_coords(jax.random.fold_in(splits[15], 71), 0),
        "leaf_order": draw_leaf_order(jax.random.fold_in(splits[15], 71), 0),
        "leaf_basis": scatter_about(splits[3], (LEAVES, K, LEAF), LEAF ** -0.5, 0.375, ((0, 128),)),
        "transfer": scatter_about(splits[4], (LEAVES, K, K), (8 * K) ** -0.5, 0.25, ((0, 128),)),
        "far_coupling": scatter_about(splits[5], (CL * N_LEAF, K, K), K ** -0.5, 0.75, ((0, 128),)),
        "far_target": place_ends(jax.random.randint(splits[6], (CL * N_LEAF,), 0, LD), jax.random.fold_in(splits[6], 1), 0, LD - 1).astype(jnp.int32),
        "far_source": draw_far_source(jax.random.fold_in(splits[15], 71), 0),
        "far_live": place_ends((jax.random.randint(splits[8], (CL * N_LEAF,), 0, 4) < 3).astype(jnp.int32), jax.random.fold_in(splits[8], 1), 0, 1),
        "top_coupling": scatter_about(splits[9], (CP * N_LEAF, K, K), K ** -0.5, 0.75, ((0, 128),)),
        "top_target": place_ends(jax.random.randint(splits[10], (CP * N_LEAF,), 0, PD), jax.random.fold_in(splits[10], 1), 0, PD - 1).astype(jnp.int32),
        "top_source": draw_top_source(jax.random.fold_in(splits[15], 71), 0),
        "top_live": place_ends((jax.random.randint(splits[12], (CP * N_LEAF,), 0, 4) < 3).astype(jnp.int32), jax.random.fold_in(splits[12], 1), 0, 1),
        "near_source": draw_near_source(jax.random.fold_in(splits[15], 71), 0),
        "near_count": draw_near_count(jax.random.fold_in(splits[15], 71), 0),
    }


delta_square = 0.0025

def kernel_values(target_pos, source_pos, live_rows, leaf_pts):
    diff_x = target_pos[0][:, None, :, None] - source_pos[0][:, :, None, :]
    diff_y = target_pos[1][:, None, :, None] - source_pos[1][:, :, None, :]
    diff_z = target_pos[2][:, None, :, None] - source_pos[2][:, :, None, :]
    squared = diff_x * diff_x + diff_y * diff_y + diff_z * diff_z
    inverse = 1.0 / (leaf_pts * jnp.sqrt(squared + delta_square))
    return jnp.where(live_rows[:, :, None, None], inverse, 0.0).astype(jnp.bfloat16)

def near_field(tree_x, tree_c, near_source, near_count):
    leaf_values = tree_x.reshape(R, LEAVES, LEAF)
    leaf_pos = tree_c.reshape(3, LEAVES, LEAF)
    near_live = jnp.arange(NEAR, dtype=jnp.int32)[None, :] < near_count[:, None]
    group_size = 8

    def per_group(group_index):
        start = group_index * group_size
        source_rows = lax.dynamic_slice_in_dim(near_source, start, group_size, 0)
        live_rows = lax.dynamic_slice_in_dim(near_live, start, group_size, 0)
        target_pos = lax.dynamic_slice_in_dim(leaf_pos, start, group_size, 1)
        source_pos = jnp.take(leaf_pos, source_rows, axis=1)
        source_vals = jnp.take(leaf_values, source_rows, axis=1)
        kernel_block = kernel_values(target_pos, source_pos, live_rows, LEAF)
        return jnp.einsum('gnij,rgnj->rgi', kernel_block.astype(jnp.float32), source_vals.astype(jnp.float32))
    stacked = lax.map(per_group, jnp.arange(LEAVES // group_size, dtype=jnp.int32))
    return stacked.transpose(1, 0, 2, 3).reshape(R, POINTS)

def couple(table, coupling, target, source, live, per_dev, count_dev):

    def couple_step(accum_far, device_id):
        start = device_id * per_dev
        coupling_rows = lax.dynamic_slice_in_dim(coupling, start, per_dev, 0)
        target_rows = lax.dynamic_slice_in_dim(target, start, per_dev, 0)
        source_rows = lax.dynamic_slice_in_dim(source, start, per_dev, 0)
        live_rows = lax.dynamic_slice_in_dim(live, start, per_dev, 0)
        source_coeff = jnp.take(table, source_rows, axis=0)
        slot_terms = jnp.einsum('skj,sjr->skr', coupling_rows.astype(jnp.float32), source_coeff.astype(jnp.float32)).astype(jnp.bfloat16)
        live_weight = jnp.where(live_rows > 0, 1.0, 0.0).astype(jnp.float32)
        accum_far = accum_far.at[device_id * count_dev + target_rows].add(slot_terms.astype(jnp.float32) * live_weight[:, None, None])
        return (accum_far, None)
    start_sum = jnp.zeros((table.shape[0], K, R), jnp.float32)
    result, unused = lax.scan(couple_step, start_sum, jnp.arange(N_LEAF, dtype=jnp.int32))
    return result

def reference(points, coords, leaf_order, leaf_basis, transfer, far_coupling, far_target, far_source, far_live, top_coupling, top_target, top_source, top_live, near_source, near_count):
    tree_x = jnp.take(points, leaf_order, axis=1)
    tree_c = jnp.take(coords, leaf_order, axis=1)
    leaf_values = tree_x.reshape(R, LEAVES, LEAF).astype(jnp.float32)
    leaf_coeff = jnp.einsum('lkp,rlp->lkr', leaf_basis.astype(jnp.float32), leaf_values).astype(jnp.bfloat16)
    upward = jnp.einsum('lkj,ljr->lkr', transfer.astype(jnp.float32), leaf_coeff.astype(jnp.float32))
    upward = upward.reshape(PARENTS, 8, K, R).sum(axis=1).astype(jnp.bfloat16)
    leaf_far = couple(leaf_coeff, far_coupling, far_target, far_source, far_live, CL, LD)
    top_far = couple(upward, top_coupling, top_target, top_source, top_live, CP, PD).astype(jnp.bfloat16)
    child_far = jnp.repeat(top_far, 8, axis=0)
    downward = jnp.einsum('lkj,lkr->ljr', transfer.astype(jnp.float32), child_far.astype(jnp.float32))
    leaf_total = (leaf_far + downward).astype(jnp.bfloat16)
    far_field = jnp.einsum('lkr,lkp->rlp', leaf_total.astype(jnp.float32), leaf_basis.astype(jnp.float32)).reshape(R, POINTS)
    near_part = near_field(tree_x, tree_c, near_source, near_count)
    summed = (far_field + near_part).astype(jnp.bfloat16)
    return jnp.zeros((R, POINTS), jnp.bfloat16).at[:, leaf_order].set(summed)
```

```python
import functools

import jax
import jax.numpy as jnp
from jax import lax
from jax.experimental import pallas as pl
from jax.experimental.pallas import tpu as pltpu
from jax.sharding import PartitionSpec as P

delta_square = 0.0025
AXIS = "leaf"
ROWS = 16
GROUP = 4
WIDE = 8
CHUNK = 32
VMEM_BYTES = 60 * 1024 * 1024
F32 = jnp.float32
BF16 = jnp.bfloat16

NT = (((1,), (1,)), ((), ()))
TN = (((0,), (0,)), ((), ()))


def mm(a, b, dims=(((1,), (0,)), ((), ()))):
    return lax.dot_general(a, b, dims, preferred_element_type=F32)


def log2(n):
    return n.bit_length() - 1


def three_parts(v):
    hi = v.astype(BF16).astype(F32)
    mid = (v - hi).astype(BF16).astype(F32)
    return hi, mid, (v - hi) - mid


def order_rows(order_ref, base, t, count=1):
    rows = [order_ref[pl.ds(2 * t + h, 1), :] for h in range(2 * count)]
    return jnp.concatenate(rows, axis=1) - base


def fetch(pairs, sems):
    copies = [pltpu.make_async_copy(src, dst, sems.at[i]) for i, (src, dst) in enumerate(pairs)]
    for copy in copies:
        copy.start()
    return copies


def tree_kernel(
    base_ref, points_hbm, coords_hbm, order_hbm, basis_hbm, transfer_hbm, far_ref, top_ref,
    tree_ref, head_ref, tail_ref, table_ref, first_ref,
    points_ref, coords_ref, order_ref, basis_ref, transfer_ref, stacked, parts, extra, sems,
):
    copies = fetch(
        [
            (order_hbm, order_ref), (coords_hbm, coords_ref), (points_hbm, points_ref),
            (basis_hbm, basis_ref), (transfer_hbm, transfer_ref),
        ],
        sems,
    )
    leaves, rank_k, pts = basis_ref.shape
    vectors = points_ref.shape[0]
    height = vectors + ROWS
    reach = head_ref.shape[0]
    base = base_ref[0]
    parts[...] = jnp.zeros(parts.shape, F32)
    for copy in copies[:3]:
        copy.wait()
    hi, mid, lo = three_parts(coords_ref[...])
    parts[0:3, :] = hi
    parts[3:6, :] = mid
    parts[6:9, :] = lo
    for q in range(leaves):
        stacked[q * height : q * height + vectors, :] = points_ref[:, q * pts : (q + 1) * pts]
        stacked[q * height + vectors : (q + 1) * height, :] = parts[
            :, q * pts : (q + 1) * pts
        ].astype(BF16)
    row_id = lax.broadcasted_iota(jnp.int32, (pts, WIDE * pts), 0)
    for copy in copies[3:]:
        copy.wait()

    def gather(g, carry):
        local = order_rows(order_ref, base, g * WIDE, WIDE)
        low = local & (pts - 1)
        high = local >> log2(pts)
        onehot = jnp.where(row_id == low, 1.0, 0.0).astype(BF16)
        spread = mm(stacked[...], onehot)
        both = jnp.zeros((height, WIDE * pts), F32)
        for q in range(leaves):
            both = jnp.where(high == q, spread[q * height : (q + 1) * height, :], both)
        both = both.astype(BF16)
        for i in range(WIDE):
            t = g * WIDE + i
            found = both[:, i * pts : (i + 1) * pts]
            tree_ref[t] = found
            twice = jnp.concatenate([found[:vectors], found[:vectors]], axis=0)
            coeff = mm(basis_ref[t], twice, NT)
            left = lax.broadcasted_iota(jnp.int32, coeff.shape, 1) < vectors
            table_ref[0, t] = jnp.where(left, coeff, 0.0).astype(BF16)
            table_ref[1, t] = jnp.where(left, 0.0, coeff).astype(BF16)
        return carry

    lax.fori_loop(0, leaves // WIDE, gather, 0)
    head_ref[...] = tree_ref[0:reach]
    tail_ref[...] = tree_ref[leaves - reach : leaves]
    half = rank_k // 2
    parents = leaves // 8
    extra[...] = jnp.zeros(extra.shape, F32)
    extra[0:1, :] = (far_ref[...] >> log2(leaves)).astype(F32)
    extra[1:2, :] = (far_ref[...] & (leaves - 1)).astype(F32)
    tops = top_ref.shape[1]
    extra[2:3, 0:tops] = (top_ref[...] >> log2(parents)).astype(F32)
    extra[3:4, 0:tops] = (top_ref[...] & (parents - 1)).astype(F32)
    packed = []
    for q in range(parents):
        total = jnp.zeros((rank_k, 2 * vectors), F32)
        for c in range(8 * q, 8 * q + 8):
            total = total + mm(transfer_ref[c], table_ref[0, c] + table_ref[1, c])
        left = lax.broadcasted_iota(jnp.int32, (half, 2 * vectors), 1) < vectors
        block = jnp.where(left, total[:half], total[half:])
        packed.append(jnp.concatenate([block, extra[...]], axis=0).astype(BF16))

    def replicate(i, carry):
        for q in range(parents):
            first_ref[parents * i + q] = packed[q]
        return carry

    lax.fori_loop(0, first_ref.shape[0] // parents, replicate, 0, unroll=4)


def send_kernel(me_ref, first_ref, table_ref, out_ref, picks, picks_s, sem):
    leaves, rank_k = table_ref.shape[1:3]
    peers, tall, lanes = first_ref.shape
    half = rank_k // 2
    asked = first_ref[:, half:tall].astype(F32)
    owner, local = asked[:, 0], asked[:, 1]
    place = lax.broadcasted_iota(jnp.int32, owner.shape, 1).astype(F32)
    mine = owner == me_ref[0].astype(F32)
    key = place * leaves + local
    first = jnp.min(jnp.where(mine, key, float(lanes * leaves)), axis=1, keepdims=True)
    last = jnp.max(jnp.where(mine, key, -1.0), axis=1, keepdims=True)
    column = lax.broadcasted_iota(jnp.int32, owner.shape, 1)
    both = jnp.where(column == 0, first, jnp.where(column == 1, last, 0.0)).T[:8]
    picks[...] = both.astype(jnp.int32) & (leaves - 1)
    copy = pltpu.make_async_copy(picks, picks_s, sem)
    copy.start()
    copy.wait()

    def fill(d, carry):
        out_ref[d] = table_ref[0, picks_s[0, d]] + table_ref[1, picks_s[1, d]]
        return carry

    lax.fori_loop(0, peers, fill, 0, unroll=8)


def gift_kernel(mine_ref, sibling_ref, first_ref, own_ref, gift_ref, sems):
    slots, half = own_ref.shape[:2]

    def start(s, carry):
        for i, (source, out) in enumerate([(mine_ref, own_ref), (sibling_ref, gift_ref)]):
            pltpu.make_async_copy(
                first_ref.at[source[s] >> 1, 0:half], out.at[s], sems.at[i]
            ).start()
        return carry

    lax.fori_loop(0, slots, start, 0, unroll=8)
    for i, out in enumerate([own_ref, gift_ref]):
        pltpu.make_async_copy(first_ref.at[0:slots, 0:half], out, sems.at[i]).wait()


def inverse_kernel(base_ref, order_ref, onehot_ref, id_ref):
    leaves, pts = onehot_ref.shape[:2]
    base = base_ref[0]
    row_id = lax.broadcasted_iota(jnp.int32, (pts, pts), 0)
    tile_id = lax.broadcasted_iota(jnp.int32, (leaves, pts), 0)
    position = lax.broadcasted_iota(jnp.int32, (leaves, pts), 1).astype(F32)

    def leaf(t, total):
        local = order_rows(order_ref, base, t)
        low = local & (pts - 1)
        high = local >> log2(pts)
        onehot = jnp.where(row_id == low, 1.0, 0.0).astype(BF16)
        here = jnp.where(tile_id == high, 1.0, 0.0)
        rows = jnp.concatenate([here * t.astype(F32), here * position], axis=0)
        return total + mm(rows.astype(BF16), onehot, NT)

    total = lax.fori_loop(0, leaves, leaf, jnp.zeros((2 * leaves, pts), F32))
    id_ref[...] = total[0:leaves].astype(jnp.int32)
    where = total[leaves:].astype(jnp.int32)
    for q in range(leaves):
        onehot_ref[q] = jnp.where(row_id == where[q : q + 1], 1.0, 0.0).astype(BF16)


def near_kernel(
    me_ref, source_ref, count_ref, left_ref, tree_ref, right_ref, out_ref,
    x_all, target_c, source_c, block_ref, weight_ref, pair_ref,
):
    leaves, height, pts = tree_ref.shape
    vectors = out_ref.shape[1]
    reach = left_ref.shape[0]
    wide = leaves + 2 * reach
    window = 2 * reach + 1
    x_all[0:reach] = left_ref[:, 0:vectors]
    x_all[reach : reach + leaves] = tree_ref[:, 0:vectors]
    x_all[reach + leaves : wide] = right_ref[:, 0:vectors]
    out_ref[...] = jnp.zeros(out_ref.shape, F32)
    lanes = source_c.shape[2] // 3
    part = lax.broadcasted_iota(jnp.int32, (ROWS, 3 * lanes), 0)
    axis_of = lax.broadcasted_iota(jnp.int32, (ROWS, 3 * lanes), 1) // lanes
    chosen = (part == axis_of) | (part == axis_of + 3) | (part == axis_of + 6)
    spread = jnp.where(chosen, float(pts), 0.0).astype(BF16)

    def prepare(ref, count, offset, own):
        def step(l, carry):
            raw = ref[l, vectors:height]
            source_c[offset + l] = mm(raw, spread, TN)
            if own:
                raw = raw.astype(F32)
                target_c[l] = (raw[0:8] + raw[3:11] + raw[6:14]) * float(pts)
            return carry

        lax.fori_loop(0, count, step, 0, unroll=2)

    prepare(left_ref, reach, 0, False)
    prepare(tree_ref, leaves, reach, True)
    prepare(right_ref, reach, reach + leaves, False)

    def tally(t, carry):
        shift = t + me_ref[0] * leaves - reach
        near, far = 0, 0
        for n in range(source_ref.shape[1]):
            m = source_ref[t, n] - shift
            live = jnp.where(count_ref[t] > n, 1, 0)
            near = near + (jnp.where(m < 8, live, 0) << (4 * (m & 7)))
            far = far + jnp.where(m < 8, 0, live)
        weight_ref[t] = near
        weight_ref[t + leaves] = far
        return carry

    lax.fori_loop(0, leaves, tally, 0, unroll=2)

    def listing(s, count):
        for m in range(window):
            t = s - m
            inside = (t >= 0) & (t < leaves)
            at = jnp.where(inside, t, 0)
            word = weight_ref[at] >> (4 * m) if m < 8 else weight_ref[at + leaves]
            weight = jnp.where(inside, word & 15, 0)
            pair_ref[count] = s + 256 * at + 65536 * weight
            count = count + jnp.where(weight > 0, 1, 0)
        pair_ref[count] = s
        return count + (count & 1)

    count = lax.fori_loop(0, wide, listing, 0)
    for i in range(2 * GROUP):
        pair_ref[count + i] = reach
    soft = delta_square * float(pts) * float(pts)

    def group(g, carry):
        for i in range(GROUP):
            n = 2 * (g * GROUP + i)
            pair = (pair_ref[n], pair_ref[n + 1])
            s = pair[0] & 255
            both = [(p >> 8) & 255 for p in pair]
            for row in range(0, pts, CHUNK):
                rows = slice(row, row + CHUNK)
                source = [source_c[s, rows, axis * lanes : (axis + 1) * lanes] for axis in range(3)]
                for h, t in enumerate(both):
                    for c in range(pts // lanes):
                        at = slice(c * lanes, (c + 1) * lanes)
                        dx, dy, dz = [target_c[t, k : k + 1, at] - source[k] for k in range(3)]
                        squared = dx * dx + dy * dy + dz * dz + soft
                        block_ref[i, rows, h * pts + c * lanes : h * pts + (c + 1) * lanes] = (
                            lax.rsqrt(squared).astype(BF16)
                        )
            product = mm(x_all[s], block_ref[i])
            for h, t in enumerate(both):
                weight = (pair[h] >> 16).astype(F32)
                out_ref[t] += weight * product[:, h * pts : (h + 1) * pts]
        return carry

    lax.fori_loop(0, (count // 2 + GROUP - 1) // GROUP, group, 0)


def top_kernel(
    me_ref, source_ref, target_ref, live_ref, coupling_ref, own_ref, other_ref, out_ref, total
):
    slots, rank_k = coupling_ref.shape[:2]
    parents, vectors = out_ref.shape[:2]
    core = me_ref[0] & (parents - 1)
    total[...] = jnp.zeros(total.shape, F32)

    def step(s, carry):
        same = (source_ref[s] & (parents - 1)) == core
        got = jnp.where(same, own_ref[s].astype(F32), other_ref[s].astype(F32))
        full = jnp.concatenate([got, pltpu.roll(got, vectors, 1)], axis=0).astype(BF16)
        term = mm(coupling_ref[s], full).astype(BF16).astype(F32)
        weight = jnp.where(live_ref[s] > 0, 1.0, 0.0)
        total[target_ref[s]] += weight * term
        return carry

    lax.fori_loop(0, slots, step, 0, unroll=8)
    for q in range(parents):
        out_ref[q] = total[q].T[:vectors].astype(BF16)


def rank_kernel(leaf_bits, source_ref, live_ref, half_ref, owner_ref, seen):
    slots = source_ref.shape[0]

    def clear(i, carry):
        seen[i] = 0
        return carry

    lax.fori_loop(0, seen.shape[0], clear, 0, unroll=8)

    def rank(s, carry):
        owner = source_ref[s] >> leaf_bits
        half_ref[s] = jnp.where(live_ref[s] > 0, seen[owner], 2)
        owner_ref[s] = owner
        seen[owner] = 1
        return carry

    lax.fori_loop(0, slots, rank, 0, unroll=8)


def finish_kernel(
    target_ref, half_ref, owner_ref,
    got_hbm, coupling_hbm, top_hbm, transfer_hbm, basis_hbm, near_hbm, onehot_hbm, id_ref,
    out_ref,
    got_ref, coupling_ref, top_ref, transfer_ref, basis_ref, near_ref, onehot_ref,
    total, summed, sems,
):
    copies = fetch(
        [
            (got_hbm, got_ref), (coupling_hbm, coupling_ref), (top_hbm, top_ref),
            (transfer_hbm, transfer_ref), (basis_hbm, basis_ref), (near_hbm, near_ref),
            (onehot_hbm, onehot_ref),
        ],
        sems,
    )
    slots, rank_k = coupling_ref.shape[:2]
    leaves, vectors, pts = near_ref.shape
    total[...] = jnp.zeros(total.shape, F32)
    side = lax.broadcasted_iota(jnp.int32, (rank_k, 2 * vectors), 1) // vectors
    for copy in copies[:2]:
        copy.wait()

    def step(s, carry):
        term = mm(coupling_ref[s], got_ref[owner_ref[s]])
        term = term.astype(BF16).astype(F32)
        total[target_ref[s]] += jnp.where(side == half_ref[s], term, 0.0)
        return carry

    lax.fori_loop(0, slots, step, 0, unroll=8)
    for copy in copies[2:]:
        copy.wait()
    for t in range(leaves):
        both = total[t]
        far = (both + pltpu.roll(both, vectors, 1)).T[:vectors]
        far = (far + mm(top_ref[t // 8], transfer_ref[t])).astype(BF16)
        value = mm(far, basis_ref[t]) + near_ref[t]
        summed[t * vectors : (t + 1) * vectors, :] = value.astype(BF16)

    def tile(g, carry):
        onehot = jnp.concatenate([onehot_ref[g * WIDE + i] for i in range(WIDE)], axis=1)
        leaf_id = jnp.concatenate([id_ref[pl.ds(g * WIDE + i, 1), :] for i in range(WIDE)], axis=1)
        spread = mm(summed[...], onehot)
        found = jnp.zeros((vectors, WIDE * pts), F32)
        for t in range(leaves):
            found = jnp.where(leaf_id == t, spread[t * vectors : (t + 1) * vectors], found)
        cols = pl.ds(pl.multiple_of(g * WIDE * pts, WIDE * pts), WIDE * pts)
        out_ref[:, cols] = found.astype(BF16)
        return carry

    lax.fori_loop(0, leaves // WIDE, tile, 0)


def smem():
    return pl.BlockSpec(memory_space=pltpu.SMEM)


def vmem():
    return pl.BlockSpec(memory_space=pltpu.VMEM)


def anywhere():
    return pl.BlockSpec(memory_space=pltpu.HBM)


def params():
    return pltpu.CompilerParams(vmem_limit_bytes=VMEM_BYTES)


def shards(
    points, coords, leaf_order, leaf_basis, transfer, far_coupling, far_target, far_source,
    far_live, top_coupling, top_target, top_source, top_live, near_source, near_count,
):
    peers = lax.axis_size(AXIS)
    me = lax.axis_index(AXIS).astype(jnp.int32)
    vectors = points.shape[0]
    leaves, rank_k, pts = leaf_basis.shape
    parents = leaves // 8
    reach = leaves // 4
    height = vectors + ROWS
    slots = far_source.shape[0]
    me_s = me.reshape(1)
    base_s = me_s * (leaves * pts)
    order = leaf_order.reshape(2 * leaves, pts // 2)
    shape = jax.ShapeDtypeStruct

    tops = top_source.shape[0]
    half = rank_k // 2
    tree, head, tail, table, first = pl.pallas_call(
        tree_kernel,
        out_shape=[
            shape((leaves, height, pts), BF16),
            shape((reach, height, pts), BF16),
            shape((reach, height, pts), BF16),
            shape((2, leaves, rank_k, 2 * vectors), BF16),
            shape((peers, half + 8, 2 * vectors), BF16),
        ],
        in_specs=[smem()] + [anywhere()] * 5 + [vmem()] * 2,
        out_specs=[vmem()] * 5,
        scratch_shapes=[
            pltpu.VMEM(points.shape, BF16),
            pltpu.VMEM(coords.shape, F32),
            pltpu.VMEM(order.shape, jnp.int32),
            pltpu.VMEM(leaf_basis.shape, BF16),
            pltpu.VMEM(transfer.shape, BF16),
            pltpu.VMEM((leaves * height, pts), BF16),
            pltpu.VMEM((ROWS, leaves * pts), F32),
            pltpu.VMEM((8, 2 * vectors), F32),
            pltpu.SemaphoreType.DMA((5,)),
        ],
        compiler_params=params(),
        name="tree",
    )(
        base_s, points, coords, order, leaf_basis, transfer,
        far_source.reshape(1, slots), top_source.reshape(1, tops),
    )
    first = lax.all_to_all(first, AXIS, 0, 0, tiled=True)
    ends = peers - 1
    left = lax.ppermute(tail, AXIS, [(i, i + 1) for i in range(ends)])
    right = lax.ppermute(head, AXIS, [(i + 1, i) for i in range(ends)])
    onehots, ids = pl.pallas_call(
        inverse_kernel,
        out_shape=[shape((leaves, pts, pts), BF16), shape((leaves, pts), jnp.int32)],
        in_specs=[smem(), vmem()],
        out_specs=[vmem(), vmem()],
        compiler_params=params(),
        name="inverse",
    )(base_s, order)
    halves, owners = pl.pallas_call(
        functools.partial(rank_kernel, log2(leaves)),
        out_shape=[shape((slots,), jnp.int32)] * 2,
        in_specs=[smem()] * 2,
        out_specs=[smem()] * 2,
        scratch_shapes=[pltpu.SMEM((peers,), jnp.int32)],
        name="rank",
    )(far_source, far_live)
    first, table, onehots, halves, left, right = lax.optimization_barrier(
        (first, table, onehots, halves, left, right)
    )
    send = pl.pallas_call(
        send_kernel,
        out_shape=shape((peers, rank_k, 2 * vectors), BF16),
        in_specs=[smem()] + [vmem()] * 2,
        out_specs=vmem(),
        scratch_shapes=[
            pltpu.VMEM((8, peers), jnp.int32),
            pltpu.SMEM((8, peers), jnp.int32),
            pltpu.SemaphoreType.DMA,
        ],
        compiler_params=params(),
        name="send",
    )(me_s, first, table)
    got = lax.all_to_all(send, AXIS, 0, 0, tiled=True)
    sibling = lax.dynamic_slice(first, (me ^ 1, half + 2, 0), (1, 2, tops))[0].astype(jnp.int32)
    sibling = sibling[0] * parents + sibling[1]
    block = shape((tops, half, 2 * vectors), BF16)
    own_blocks, gift = pl.pallas_call(
        gift_kernel,
        out_shape=[block, block],
        in_specs=[smem(), smem(), anywhere()],
        out_specs=[vmem(), vmem()],
        scratch_shapes=[pltpu.SemaphoreType.DMA((2,))],
        compiler_params=params(),
        name="gift",
    )(top_source, sibling, first)
    other_blocks = lax.ppermute(gift, AXIS, [(i, i ^ 1) for i in range(peers)])
    near = pl.pallas_call(
        near_kernel,
        out_shape=shape((leaves, vectors, pts), F32),
        in_specs=[smem()] * 3 + [vmem()] * 3,
        out_specs=vmem(),
        scratch_shapes=[
            pltpu.VMEM((leaves + 2 * reach, vectors, pts), BF16),
            pltpu.VMEM((leaves, 8, pts), F32),
            pltpu.VMEM((leaves + 2 * reach, pts, 3 * 128), F32),
            pltpu.VMEM((GROUP, pts, 2 * pts), BF16),
            pltpu.SMEM((2 * leaves,), jnp.int32),
            pltpu.SMEM(((2 * reach + 2) * (leaves + 2 * reach) + 2 * GROUP + 2,), jnp.int32),
        ],
        compiler_params=params(),
        name="near",
    )(me_s, near_source, near_count, left, tree, right)
    top_far = pl.pallas_call(
        top_kernel,
        out_shape=shape((parents, vectors, rank_k), BF16),
        in_specs=[smem()] * 4 + [vmem()] * 3,
        out_specs=vmem(),
        scratch_shapes=[pltpu.VMEM((parents, rank_k, 2 * vectors), F32)],
        compiler_params=params(),
        name="top",
    )(me_s, top_source, top_target, top_live, top_coupling, own_blocks, other_blocks)
    got, near, top_far = lax.optimization_barrier((got, near, top_far))
    return pl.pallas_call(
        finish_kernel,
        out_shape=shape((vectors, leaves * pts), BF16),
        in_specs=[smem()] * 3 + [anywhere()] * 7 + [vmem()],
        out_specs=vmem(),
        scratch_shapes=[
            pltpu.VMEM(got.shape, BF16),
            pltpu.VMEM(far_coupling.shape, BF16),
            pltpu.VMEM(top_far.shape, BF16),
            pltpu.VMEM(transfer.shape, BF16),
            pltpu.VMEM(leaf_basis.shape, BF16),
            pltpu.VMEM(near.shape, F32),
            pltpu.VMEM(onehots.shape, BF16),
            pltpu.VMEM((leaves, rank_k, 2 * vectors), F32),
            pltpu.VMEM((leaves * vectors, pts), BF16),
            pltpu.SemaphoreType.DMA((7,)),
        ],
        compiler_params=params(),
        name="finish",
    )(
        far_target, halves, owners,
        got, far_coupling, top_far, transfer, leaf_basis, near, onehots, ids,
    )


def solution(mesh):
    placed = (
        P(None, AXIS), P(None, AXIS), P(AXIS), P(AXIS, None, None), P(AXIS, None, None),
        P(AXIS, None, None), P(AXIS), P(AXIS), P(AXIS), P(AXIS, None, None), P(AXIS), P(AXIS),
        P(AXIS), P(AXIS, None), P(AXIS),
    )
    return jax.shard_map(
        shards, mesh=mesh, in_specs=placed, out_specs=P(None, AXIS), check_vma=False
    )
```

```python
import functools

import jax
import jax.numpy as jnp
from jax import lax
from jax.experimental import pallas as pl
from jax.experimental.pallas import tpu as pltpu
from jax.sharding import PartitionSpec as P

delta_square = 0.0025
AXIS = "leaf"
ROWS = 16
GROUP = 4
WIDE = 8
CHUNK = 32
REPEAT = 16
UNROLL = 32
MOST_VMEM = 60 * 1024 * 1024
SOME_VMEM = 40 * 1024 * 1024
SEND_VMEM = SOME_VMEM
LAST_VMEM = 61 * 1024 * 1024
F32 = jnp.float32
BF16 = jnp.bfloat16

NT = (((1,), (1,)), ((), ()))
TN = (((0,), (0,)), ((), ()))


def mm(a, b, dims=(((1,), (0,)), ((), ()))):
    return lax.dot_general(a, b, dims, preferred_element_type=F32)


def log2(n):
    return n.bit_length() - 1


def three_parts(v):
    hi = v.astype(BF16).astype(F32)
    mid = (v - hi).astype(BF16).astype(F32)
    return hi, mid, (v - hi) - mid


def order_rows(order_ref, base, t, count=1):
    rows = [order_ref[pl.ds(2 * t + h, 1), :] for h in range(2 * count)]
    return jnp.concatenate(rows, axis=1) - base


def fetch(pairs, sems):
    copies = [pltpu.make_async_copy(src, dst, sems.at[i]) for i, (src, dst) in enumerate(pairs)]
    for copy in copies:
        copy.start()
    return copies


def tree_kernel(
    base_ref, points_hbm, coords_hbm, order_hbm, basis_hbm, transfer_hbm, far_ref, top_ref,
    tree_hbm, head_hbm, tail_hbm, table_hbm, first_hbm,
    points_ref, coords_ref, order_ref, basis_ref, transfer_ref, stacked, parts, extra, sems,
    tree_ref, table_ref, first_ref, upward, out_sems, first_sem,
):
    copies = fetch(
        [
            (order_hbm, order_ref), (coords_hbm, coords_ref), (points_hbm, points_ref),
            (basis_hbm, basis_ref), (transfer_hbm, transfer_ref),
        ],
        sems,
    )
    leaves, rank_k, pts = basis_ref.shape
    vectors = points_ref.shape[0]
    height = vectors + ROWS
    reach = head_hbm.shape[0]
    base = base_ref[0]
    parts[...] = jnp.zeros(parts.shape, F32)
    for copy in copies[:3]:
        copy.wait()
    hi, mid, lo = three_parts(coords_ref[...])
    parts[0:3, :] = hi
    parts[3:6, :] = mid
    parts[6:9, :] = lo
    for q in range(leaves):
        stacked[q * height : q * height + vectors, :] = points_ref[:, q * pts : (q + 1) * pts]
        stacked[q * height + vectors : (q + 1) * height, :] = parts[
            :, q * pts : (q + 1) * pts
        ].astype(BF16)
    row_id = lax.broadcasted_iota(jnp.int32, (pts, WIDE * pts), 0)
    for copy in copies[3:]:
        copy.wait()

    def gather(g, carry):
        local = order_rows(order_ref, base, g * WIDE, WIDE)
        low = local & (pts - 1)
        high = local >> log2(pts)
        onehot = jnp.where(row_id == low, 1.0, 0.0).astype(BF16)
        spread = mm(stacked[...], onehot)
        both = jnp.zeros((height, WIDE * pts), F32)
        for q in range(leaves):
            both = jnp.where(high == q, spread[q * height : (q + 1) * height, :], both)
        both = both.astype(BF16)
        for i in range(WIDE):
            t = g * WIDE + i
            found = both[:, i * pts : (i + 1) * pts]
            tree_ref[t] = found
            twice = jnp.concatenate([found[:vectors], found[:vectors]], axis=0)
            coeff = mm(basis_ref[t], twice, NT)
            left = lax.broadcasted_iota(jnp.int32, coeff.shape, 1) < vectors
            table_ref[0, t] = jnp.where(left, coeff, 0.0).astype(BF16)
            table_ref[1, t] = jnp.where(left, 0.0, coeff).astype(BF16)
            coeff = coeff.astype(BF16)
        return carry

    lax.fori_loop(0, leaves // WIDE, gather, 0)
    out_copies = fetch(
        [
            (table_ref, table_hbm), (tree_ref, tree_hbm), (tree_ref.at[0:reach], head_hbm),
            (tree_ref.at[leaves - reach : leaves], tail_hbm),
        ],
        out_sems,
    )
    half = rank_k // 2
    parents = leaves // 8
    extra[...] = jnp.zeros(extra.shape, F32)
    extra[0:1, :] = (far_ref[...] >> log2(leaves)).astype(F32)
    extra[1:2, :] = (far_ref[...] & (leaves - 1)).astype(F32)
    tops = top_ref.shape[1]
    extra[2:3, 0:tops] = (top_ref[...] >> log2(parents)).astype(F32)
    extra[3:4, 0:tops] = (top_ref[...] & (parents - 1)).astype(F32)
    packed = []
    for q in range(parents):
        total = jnp.zeros((rank_k, 2 * vectors), F32)
        for c in range(8 * q, 8 * q + 8):
            total = total + mm(transfer_ref[c], table_ref[0, c] + table_ref[1, c])
        left = lax.broadcasted_iota(jnp.int32, (half, 2 * vectors), 1) < vectors
        block = jnp.where(left, total[:half], total[half:])
        packed.append(jnp.concatenate([block, extra[...]], axis=0).astype(BF16))

    part = first_ref.shape[0]
    for i in range(part // parents):
        for q in range(parents):
            first_ref[parents * i + q] = packed[q]
    peers = first_hbm.shape[0]
    for i in range(peers // part):
        pltpu.make_async_copy(
            first_ref, first_hbm.at[i * part : (i + 1) * part], first_sem.at[i]
        ).start()
    for i in range(peers // part):
        pltpu.make_async_copy(
            first_ref, first_hbm.at[i * part : (i + 1) * part], first_sem.at[i]
        ).wait()
    for copy in out_copies:
        copy.wait()


def send_kernel(
    me_ref, first_ref, table_hbm, out_hbm, table_ref, out_ref, picks, picks_s, sem, table_sem, sems
):
    table_copy = pltpu.make_async_copy(table_hbm, table_ref, table_sem)
    table_copy.start()
    leaves, rank_k = table_ref.shape[1:3]
    peers, tall, lanes = first_ref.shape
    half = rank_k // 2
    asked = first_ref[:, half:tall].astype(F32)
    owner, local = asked[:, 0], asked[:, 1]
    place = lax.broadcasted_iota(jnp.int32, owner.shape, 1).astype(F32)
    mine = owner == me_ref[0].astype(F32)
    key = place * leaves + local
    first = jnp.min(jnp.where(mine, key, float(lanes * leaves)), axis=1, keepdims=True)
    last = jnp.max(jnp.where(mine, key, -1.0), axis=1, keepdims=True)
    column = lax.broadcasted_iota(jnp.int32, owner.shape, 1)
    both = jnp.where(column == 0, first, jnp.where(column == 1, last, 0.0)).T[:8]
    picks[...] = both.astype(jnp.int32) & (leaves - 1)
    copy = pltpu.make_async_copy(picks, picks_s, sem)
    copy.start()
    copy.wait()

    def fill(d, carry):
        out_ref[d] = table_ref[0, picks_s[0, d]] + table_ref[1, picks_s[1, d]]
        return carry

    table_copy.wait()
    pieces = sems.shape[0]
    part = peers // pieces
    copies = []
    for i in range(pieces):
        span = slice(i * part, (i + 1) * part)
        lax.fori_loop(i * part, (i + 1) * part, fill, 0, unroll=8)
        copies.append(pltpu.make_async_copy(out_ref.at[span], out_hbm.at[span], sems.at[i]))
        copies[-1].start()
    for copy in copies:
        copy.wait()


def gift_kernel(mine_ref, sibling_ref, first_ref, own_ref, gift_ref, sems):
    slots, half = own_ref.shape[:2]

    def start(s, carry):
        for i, (source, out) in enumerate([(mine_ref, own_ref), (sibling_ref, gift_ref)]):
            pltpu.make_async_copy(
                first_ref.at[source[s] >> 1, 0:half], out.at[s], sems.at[i]
            ).start()
        return carry

    lax.fori_loop(0, slots, start, 0, unroll=8)
    for i, out in enumerate([own_ref, gift_ref]):
        pltpu.make_async_copy(first_ref.at[0:slots, 0:half], out, sems.at[i]).wait()


def inverse_kernel(base_ref, order_ref, id_ref, place_ref):
    leaves, pts = id_ref.shape
    base = base_ref[0]
    row_id = lax.broadcasted_iota(jnp.int32, (pts, pts), 0)
    tile_id = lax.broadcasted_iota(jnp.int32, (leaves, pts), 0)
    position = lax.broadcasted_iota(jnp.int32, (leaves, pts), 1).astype(F32)

    def leaf(t, total):
        local = order_rows(order_ref, base, t)
        low = local & (pts - 1)
        high = local >> log2(pts)
        onehot = jnp.where(row_id == low, 1.0, 0.0).astype(BF16)
        here = jnp.where(tile_id == high, 1.0, 0.0)
        rows = jnp.concatenate([here * t.astype(F32), here * position], axis=0)
        return total + mm(rows.astype(BF16), onehot, NT)

    total = lax.fori_loop(0, leaves, leaf, jnp.zeros((2 * leaves, pts), F32), unroll=4)
    id_ref[...] = total[0:leaves].astype(jnp.int32)
    place_ref[...] = total[leaves:].astype(jnp.int32)


def near_kernel(
    me_ref, source_ref, count_ref, left_ref, tree_ref, right_ref, out_ref,
    x_all, target_c, source_c, block_ref, weight_ref, pair_ref,
):
    leaves, height, pts = tree_ref.shape
    vectors = out_ref.shape[1]
    reach = left_ref.shape[0]
    wide = leaves + 2 * reach
    window = 2 * reach + 1
    x_all[0:reach] = left_ref[:, 0:vectors]
    x_all[reach : reach + leaves] = tree_ref[:, 0:vectors]
    x_all[reach + leaves : wide] = right_ref[:, 0:vectors]
    out_ref[...] = jnp.zeros(out_ref.shape, F32)
    lanes = source_c.shape[2] // 3
    part = lax.broadcasted_iota(jnp.int32, (ROWS, 3 * lanes), 0)
    axis_of = lax.broadcasted_iota(jnp.int32, (ROWS, 3 * lanes), 1) // lanes
    chosen = (part == axis_of) | (part == axis_of + 3) | (part == axis_of + 6)
    spread = jnp.where(chosen, float(pts), 0.0).astype(BF16)

    def prepare(ref, count, offset, own):
        def step(l, carry):
            raw = ref[l, vectors:height]
            source_c[offset + l] = mm(raw, spread, TN)
            if own:
                raw = raw.astype(F32)
                target_c[l] = (raw[0:8] + raw[3:11] + raw[6:14]) * float(pts)
            return carry

        lax.fori_loop(0, count, step, 0, unroll=2)

    prepare(left_ref, reach, 0, False)
    prepare(tree_ref, leaves, reach, True)
    prepare(right_ref, reach, reach + leaves, False)

    def tally(t, carry):
        shift = t + me_ref[0] * leaves - reach
        near, far = 0, 0
        for n in range(source_ref.shape[1]):
            m = source_ref[t, n] - shift
            live = jnp.where(count_ref[t] > n, 1, 0)
            near = near + (jnp.where(m < 8, live, 0) << (4 * (m & 7)))
            far = far + jnp.where(m < 8, 0, live)
        weight_ref[t] = near
        weight_ref[t + leaves] = far
        return carry

    lax.fori_loop(0, leaves, tally, 0, unroll=2)

    def listing(s, count):
        for m in range(window):
            t = s - m
            inside = (t >= 0) & (t < leaves)
            at = jnp.where(inside, t, 0)
            word = weight_ref[at] >> (4 * m) if m < 8 else weight_ref[at + leaves]
            weight = jnp.where(inside, word & 15, 0)
            pair_ref[count] = s + 256 * at + 65536 * weight
            count = count + jnp.where(weight > 0, 1, 0)
        pair_ref[count] = s
        return count + (count & 1)

    count = lax.fori_loop(0, wide, listing, 0)
    for i in range(2 * GROUP):
        pair_ref[count + i] = reach
    soft = delta_square * float(pts) * float(pts)

    def group(g, carry):
        for i in range(GROUP):
            n = 2 * (g * GROUP + i)
            pair = (pair_ref[n], pair_ref[n + 1])
            s = pair[0] & 255
            both = [(p >> 8) & 255 for p in pair]
            for row in range(0, pts, CHUNK):
                rows = slice(row, row + CHUNK)
                source = [source_c[s, rows, axis * lanes : (axis + 1) * lanes] for axis in range(3)]
                for h, t in enumerate(both):
                    for c in range(pts // lanes):
                        at = slice(c * lanes, (c + 1) * lanes)
                        dx, dy, dz = [target_c[t, k : k + 1, at] - source[k] for k in range(3)]
                        squared = dx * dx + dy * dy + dz * dz + soft
                        block_ref[i, rows, h * pts + c * lanes : h * pts + (c + 1) * lanes] = (
                            lax.rsqrt(squared).astype(BF16)
                        )
            product = mm(x_all[s], block_ref[i])
            for h, t in enumerate(both):
                weight = (pair[h] >> 16).astype(F32)
                out_ref[t] += weight * product[:, h * pts : (h + 1) * pts]
        return carry

    lax.fori_loop(0, (count // 2 + GROUP - 1) // GROUP, group, 0)


def top_kernel(
    me_ref, source_ref, target_ref, live_ref, coupling_ref, own_ref, other_ref, out_ref, total
):
    slots, rank_k = coupling_ref.shape[:2]
    parents, vectors = out_ref.shape[:2]
    core = me_ref[0] & (parents - 1)
    total[...] = jnp.zeros(total.shape, F32)

    def step(s, carry):
        same = (source_ref[s] & (parents - 1)) == core
        got = jnp.where(same, own_ref[s].astype(F32), other_ref[s].astype(F32))
        full = jnp.concatenate([got, pltpu.roll(got, vectors, 1)], axis=0).astype(BF16)
        term = mm(coupling_ref[s], full).astype(BF16).astype(F32)
        weight = jnp.where(live_ref[s] > 0, 1.0, 0.0)
        total[target_ref[s]] += weight * term
        return carry

    lax.fori_loop(0, slots, step, 0, unroll=8)
    for q in range(parents):
        out_ref[q] = total[q].T[:vectors].astype(BF16)


def rank_kernel(
    leaf_bits, source_ref, live_ref, coupling_ref, half_ref, owner_ref, coupling_out, seen
):
    slots = source_ref.shape[0]
    coupling_out[...] = coupling_ref[...]

    def clear(i, carry):
        seen[i] = 0
        return carry

    lax.fori_loop(0, seen.shape[0], clear, 0, unroll=8)

    def rank(s, carry):
        owner = source_ref[s] >> leaf_bits
        half_ref[s] = jnp.where(live_ref[s] > 0, seen[owner], 2)
        owner_ref[s] = owner
        seen[owner] = 1
        return carry

    lax.fori_loop(0, slots, rank, 0, unroll=8)


def finish_kernel(
    target_ref, half_ref, owner_ref,
    got_ref, coupling_hbm, top_hbm, transfer_hbm, basis_hbm, near_ref, id_ref, place_ref,
    out_hbm,
    coupling_ref, top_ref, transfer_ref, basis_ref, onehot_ref,
    total, summed, out_ref, sems, out_sems, coupling_sems,
):
    pieces = coupling_sems.shape[0]
    part = coupling_ref.shape[0] // pieces
    spans = [slice(i * part, (i + 1) * part) for i in range(pieces)]
    coupling_copies = fetch(
        [(coupling_hbm.at[span], coupling_ref.at[span]) for span in spans], coupling_sems
    )
    copies = fetch(
        [
            (top_hbm, top_ref), (transfer_hbm, transfer_ref), (basis_hbm, basis_ref),
        ],
        sems,
    )
    slots, rank_k = coupling_ref.shape[:2]
    leaves, vectors, pts = near_ref.shape
    total[...] = jnp.zeros(total.shape, F32)
    side = lax.broadcasted_iota(jnp.int32, (rank_k, 2 * vectors), 1) // vectors
    row_id = lax.broadcasted_iota(jnp.int32, (pts, pts), 0)
    for q in range(leaves):
        hot = jnp.where(row_id == place_ref[q : q + 1], 1.0, 0.0)
        onehot_ref[:, q * pts : (q + 1) * pts] = hot.astype(BF16)

    def step(s, carry):
        term = mm(coupling_ref[s], got_ref[owner_ref[s]])
        term = term.astype(BF16).astype(F32)
        total[target_ref[s]] += jnp.where(side == half_ref[s], term, 0.0)
        return carry

    for span, copy in zip(spans, coupling_copies):
        copy.wait()
        lax.fori_loop(span.start, span.stop, step, 0, unroll=UNROLL)
    for copy in copies:
        copy.wait()
    for t in range(leaves):
        both = total[t]
        far = (both + pltpu.roll(both, vectors, 1)).T[:vectors]
        far = (far + mm(top_ref[t // 8], transfer_ref[t])).astype(BF16)
        value = mm(far, basis_ref[t]) + near_ref[t]
        summed[t * vectors : (t + 1) * vectors, :] = value.astype(BF16)

    out_copies = []
    for g in range(leaves // WIDE):
        leaf_id = jnp.concatenate([id_ref[g * WIDE + i : g * WIDE + i + 1] for i in range(WIDE)], axis=1)
        cols = slice(g * WIDE * pts, (g + 1) * WIDE * pts)
        spread = mm(summed[...], onehot_ref[:, cols])
        found = jnp.zeros((vectors, WIDE * pts), F32)
        for t in range(leaves):
            found = jnp.where(leaf_id == t, spread[t * vectors : (t + 1) * vectors], found)
        out_ref[:, cols] = found.astype(BF16)
        copy = pltpu.make_async_copy(out_ref.at[:, cols], out_hbm.at[:, cols], out_sems.at[g])
        copy.start()
        out_copies.append(copy)
    for copy in out_copies:
        copy.wait()


def smem():
    return pl.BlockSpec(memory_space=pltpu.SMEM)


def vmem():
    return pl.BlockSpec(memory_space=pltpu.VMEM)


def anywhere():
    return pl.BlockSpec(memory_space=pltpu.HBM)


def busy(microseconds):
    return pl.CostEstimate(
        flops=microseconds * 10**9, bytes_accessed=10**6, transcendentals=0
    )


def params(limit=SOME_VMEM):
    return pltpu.CompilerParams(vmem_limit_bytes=limit)


def shards(
    points, coords, leaf_order, leaf_basis, transfer, far_coupling, far_target, far_source,
    far_live, top_coupling, top_target, top_source, top_live, near_source, near_count,
):
    peers = lax.axis_size(AXIS)
    me = lax.axis_index(AXIS).astype(jnp.int32)
    vectors = points.shape[0]
    leaves, rank_k, pts = leaf_basis.shape
    parents = leaves // 8
    reach = leaves // 4
    height = vectors + ROWS
    slots = far_source.shape[0]
    me_s = me.reshape(1)
    base_s = me_s * (leaves * pts)
    order = leaf_order.reshape(2 * leaves, pts // 2)
    shape = jax.ShapeDtypeStruct

    tops = top_source.shape[0]
    half = rank_k // 2
    tree, head, tail, table, first = pl.pallas_call(
        tree_kernel,
        out_shape=[
            shape((leaves, height, pts), BF16),
            shape((reach, height, pts), BF16),
            shape((reach, height, pts), BF16),
            shape((2, leaves, rank_k, 2 * vectors), BF16),
            shape((peers, half + 8, 2 * vectors), BF16),
        ],
        in_specs=[smem()] + [anywhere()] * 5 + [vmem()] * 2,
        out_specs=[anywhere()] * 5,
        scratch_shapes=[
            pltpu.VMEM(points.shape, BF16),
            pltpu.VMEM(coords.shape, F32),
            pltpu.VMEM(order.shape, jnp.int32),
            pltpu.VMEM(leaf_basis.shape, BF16),
            pltpu.VMEM(transfer.shape, BF16),
            pltpu.VMEM((leaves * height, pts), BF16),
            pltpu.VMEM((ROWS, leaves * pts), F32),
            pltpu.VMEM((8, 2 * vectors), F32),
            pltpu.SemaphoreType.DMA((5,)),
            pltpu.VMEM((leaves, height, pts), BF16),
            pltpu.VMEM((2, leaves, rank_k, 2 * vectors), BF16),
            pltpu.VMEM((REPEAT, half + 8, 2 * vectors), BF16),
            pltpu.VMEM((parents, rank_k, 2 * vectors), F32),
            pltpu.SemaphoreType.DMA((4,)),
            pltpu.SemaphoreType.DMA((peers // REPEAT,)),
        ],
        compiler_params=params(MOST_VMEM),
        cost_estimate=busy(7),
        name="tree",
    )(
        base_s, points, coords, order, leaf_basis, transfer,
        far_source.reshape(1, slots), top_source.reshape(1, tops),
    )
    first = lax.all_to_all(first, AXIS, 0, 0, tiled=True)
    ends = peers - 1
    left = lax.ppermute(tail, AXIS, [(i, i + 1) for i in range(ends)])
    right = lax.ppermute(head, AXIS, [(i + 1, i) for i in range(ends)])
    ids, places = pl.pallas_call(
        inverse_kernel,
        out_shape=[shape((leaves, pts), jnp.int32)] * 2,
        in_specs=[smem(), vmem()],
        out_specs=[vmem(), vmem()],
        compiler_params=params(),
        cost_estimate=busy(3),
        name="inverse",
    )(base_s, order)
    halves, owners, coupling = pl.pallas_call(
        functools.partial(rank_kernel, log2(leaves)),
        out_shape=[shape((slots,), jnp.int32)] * 2 + [shape(far_coupling.shape, BF16)],
        in_specs=[smem()] * 2 + [vmem()],
        out_specs=[smem()] * 2 + [vmem()],
        scratch_shapes=[pltpu.SMEM((peers,), jnp.int32)],
        compiler_params=params(MOST_VMEM),
        cost_estimate=busy(3),
        name="rank",
    )(far_source, far_live, far_coupling)
    first, table, places, coupling, left, right = lax.optimization_barrier(
        (first, table, places, coupling, left, right)
    )
    send = pl.pallas_call(
        send_kernel,
        out_shape=shape((peers, rank_k, 2 * vectors), BF16),
        in_specs=[smem(), vmem(), anywhere()],
        out_specs=anywhere(),
        scratch_shapes=[
            pltpu.VMEM(table.shape, BF16),
            pltpu.VMEM((peers, rank_k, 2 * vectors), BF16),
            pltpu.VMEM((8, peers), jnp.int32),
            pltpu.SMEM((8, peers), jnp.int32),
            pltpu.SemaphoreType.DMA,
            pltpu.SemaphoreType.DMA,
            pltpu.SemaphoreType.DMA((4,)),
        ],
        compiler_params=params(SEND_VMEM),
        cost_estimate=busy(2),
        name="send",
    )(me_s, first, table)
    got = lax.all_to_all(send, AXIS, 0, 0, tiled=True)
    sibling = lax.dynamic_slice(first, (me ^ 1, half + 2, 0), (1, 2, tops))[0].astype(jnp.int32)
    sibling = sibling[0] * parents + sibling[1]
    block = shape((tops, half, 2 * vectors), BF16)
    own_blocks, gift = pl.pallas_call(
        gift_kernel,
        out_shape=[block, block],
        in_specs=[smem(), smem(), vmem()],
        out_specs=[vmem(), vmem()],
        scratch_shapes=[pltpu.SemaphoreType.DMA((2,))],
        compiler_params=params(),
        cost_estimate=busy(2),
        name="gift",
    )(top_source, sibling, first)
    other_blocks = lax.ppermute(gift, AXIS, [(i, i ^ 1) for i in range(peers)])
    near = pl.pallas_call(
        near_kernel,
        out_shape=shape((leaves, vectors, pts), F32),
        in_specs=[smem()] * 3 + [vmem()] * 3,
        out_specs=vmem(),
        scratch_shapes=[
            pltpu.VMEM((leaves + 2 * reach, vectors, pts), BF16),
            pltpu.VMEM((leaves, 8, pts), F32),
            pltpu.VMEM((leaves + 2 * reach, pts, 3 * 128), F32),
            pltpu.VMEM((GROUP, pts, 2 * pts), BF16),
            pltpu.SMEM((2 * leaves,), jnp.int32),
            pltpu.SMEM(((2 * reach + 2) * (leaves + 2 * reach) + 2 * GROUP + 2,), jnp.int32),
        ],
        compiler_params=params(),
        cost_estimate=busy(19),
        name="near",
    )(me_s, near_source, near_count, left, tree, right)
    top_far = pl.pallas_call(
        top_kernel,
        out_shape=shape((parents, vectors, rank_k), BF16),
        in_specs=[smem()] * 4 + [vmem()] * 3,
        out_specs=vmem(),
        scratch_shapes=[pltpu.VMEM((parents, rank_k, 2 * vectors), F32)],
        compiler_params=params(),
        cost_estimate=busy(2),
        name="top",
    )(me_s, top_source, top_target, top_live, top_coupling, own_blocks, other_blocks)
    got, near, top_far = lax.optimization_barrier((got, near, top_far))
    return pl.pallas_call(
        finish_kernel,
        out_shape=shape((vectors, leaves * pts), BF16),
        in_specs=[smem()] * 3 + [vmem()] + [anywhere()] * 4 + [vmem()] * 3,
        out_specs=anywhere(),
        scratch_shapes=[
            pltpu.VMEM(coupling.shape, BF16),
            pltpu.VMEM(top_far.shape, BF16),
            pltpu.VMEM(transfer.shape, BF16),
            pltpu.VMEM(leaf_basis.shape, BF16),
            pltpu.VMEM((pts, leaves * pts), BF16),
            pltpu.VMEM((leaves, rank_k, 2 * vectors), F32),
            pltpu.VMEM((leaves * vectors, pts), BF16),
            pltpu.VMEM((vectors, leaves * pts), BF16),
            pltpu.SemaphoreType.DMA((3,)),
            pltpu.SemaphoreType.DMA((leaves // WIDE,)),
            pltpu.SemaphoreType.DMA((4,)),
        ],
        compiler_params=params(LAST_VMEM),
        cost_estimate=busy(8),
        name="finish",
    )(
        far_target, halves, owners,
        got, coupling, top_far, transfer, leaf_basis, near, ids, places,
    )


def solution(mesh):
    placed = (
        P(None, AXIS), P(None, AXIS), P(AXIS), P(AXIS, None, None), P(AXIS, None, None),
        P(AXIS, None, None), P(AXIS), P(AXIS), P(AXIS), P(AXIS, None, None), P(AXIS), P(AXIS),
        P(AXIS), P(AXIS, None), P(AXIS),
    )
    return jax.shard_map(
        shards, mesh=mesh, in_specs=placed, out_specs=P(None, AXIS), check_vma=False
    )
```

```python
import functools

import jax
import jax.numpy as jnp
from jax import lax
from jax.experimental import pallas as pl
from jax.experimental.pallas import tpu as pltpu
from jax.sharding import PartitionSpec as P

delta_square = 0.0025
AXIS = "leaf"
ROWS = 16
GROUP = 4
WIDE = 8
CHUNK = 32
REPEAT = 16
UNROLL = 16
MOST_VMEM = 60 * 1024 * 1024
SOME_VMEM = 40 * 1024 * 1024
SEND_VMEM = SOME_VMEM
LAST_VMEM = 61 * 1024 * 1024
F32 = jnp.float32
BF16 = jnp.bfloat16

NT = (((1,), (1,)), ((), ()))
TN = (((0,), (0,)), ((), ()))


def mm(a, b, dims=(((1,), (0,)), ((), ()))):
    return lax.dot_general(a, b, dims, preferred_element_type=F32)


def log2(n):
    return n.bit_length() - 1


def three_parts(v):
    hi = v.astype(BF16).astype(F32)
    mid = (v - hi).astype(BF16).astype(F32)
    return hi, mid, (v - hi) - mid


def order_rows(order_ref, base, t, count=1):
    rows = [order_ref[pl.ds(2 * t + h, 1), :] for h in range(2 * count)]
    return jnp.concatenate(rows, axis=1) - base


def fetch(pairs, sems):
    copies = [pltpu.make_async_copy(src, dst, sems.at[i]) for i, (src, dst) in enumerate(pairs)]
    for copy in copies:
        copy.start()
    return copies


def tree_kernel(
    base_ref, points_hbm, coords_hbm, order_hbm, basis_hbm, transfer_hbm, far_ref, top_ref,
    tree_hbm, head_hbm, tail_hbm, table_hbm, first_hbm,
    points_ref, coords_ref, order_ref, basis_ref, transfer_ref, stacked, parts, extra, sems,
    tree_ref, table_ref, first_ref, out_sems, first_sem,
):
    copies = fetch(
        [
            (order_hbm, order_ref), (coords_hbm, coords_ref), (points_hbm, points_ref),
            (basis_hbm, basis_ref), (transfer_hbm, transfer_ref),
        ],
        sems,
    )
    leaves, rank_k, pts = basis_ref.shape
    vectors = points_ref.shape[0]
    height = vectors + ROWS
    reach = head_hbm.shape[0]
    base = base_ref[0]
    parts[...] = jnp.zeros(parts.shape, F32)
    for copy in copies[:3]:
        copy.wait()
    hi, mid, lo = three_parts(coords_ref[...])
    parts[0:3, :] = hi
    parts[3:6, :] = mid
    parts[6:9, :] = lo
    for q in range(leaves):
        stacked[q * height : q * height + vectors, :] = points_ref[:, q * pts : (q + 1) * pts]
        stacked[q * height + vectors : (q + 1) * height, :] = parts[
            :, q * pts : (q + 1) * pts
        ].astype(BF16)
    row_id = lax.broadcasted_iota(jnp.int32, (pts, WIDE * pts), 0)
    for copy in copies[3:]:
        copy.wait()

    def gather(g, carry):
        local = order_rows(order_ref, base, g * WIDE, WIDE)
        low = local & (pts - 1)
        high = local >> log2(pts)
        onehot = jnp.where(row_id == low, 1.0, 0.0).astype(BF16)
        spread = mm(stacked[...], onehot)
        both = jnp.zeros((height, WIDE * pts), F32)
        for q in range(leaves):
            both = jnp.where(high == q, spread[q * height : (q + 1) * height, :], both)
        both = both.astype(BF16)
        for i in range(WIDE):
            t = g * WIDE + i
            found = both[:, i * pts : (i + 1) * pts]
            tree_ref[t] = found
            twice = jnp.concatenate([found[:vectors], found[:vectors]], axis=0)
            coeff = mm(basis_ref[t], twice, NT)
            left = lax.broadcasted_iota(jnp.int32, coeff.shape, 1) < vectors
            table_ref[0, t] = jnp.where(left, coeff, 0.0).astype(BF16)
            table_ref[1, t] = jnp.where(left, 0.0, coeff).astype(BF16)
            coeff = coeff.astype(BF16)
        return carry

    half = rank_k // 2
    parents = leaves // 8
    extra[...] = jnp.zeros(extra.shape, F32)
    extra[0:1, :] = (far_ref[...] >> log2(leaves)).astype(F32)
    extra[1:2, :] = (far_ref[...] & (leaves - 1)).astype(F32)
    tops = top_ref.shape[1]
    extra[2:3, 0:tops] = (top_ref[...] >> log2(parents)).astype(F32)
    extra[3:4, 0:tops] = (top_ref[...] & (parents - 1)).astype(F32)
    repeat, couples = first_ref.shape[1], first_hbm.shape[0]
    parent_copies = []
    for q in range(parents):
        for g in range(8 * q // WIDE, max(8 * (q + 1) // WIDE, 8 * q // WIDE + 1)):
            gather(g, 0)
        total = jnp.zeros((rank_k, 2 * vectors), F32)
        for c in range(8 * q, 8 * q + 8):
            total = total + mm(transfer_ref[c], table_ref[0, c] + table_ref[1, c])
        left = lax.broadcasted_iota(jnp.int32, (half, 2 * vectors), 1) < vectors
        block = jnp.where(left, total[:half], total[half:])
        block = jnp.concatenate([block, extra[...]], axis=0).astype(BF16)
        for i in range(repeat):
            first_ref[q, i] = block
        parent_copies += fetch(
            [
                (first_ref.at[q], first_hbm.at[i * repeat : (i + 1) * repeat, q])
                for i in range(couples // repeat)
            ],
            first_sem.at[q],
        )
    out_copies = fetch(
        [
            (table_ref, table_hbm), (tree_ref, tree_hbm), (tree_ref.at[0:reach], head_hbm),
            (tree_ref.at[leaves - reach : leaves], tail_hbm),
        ],
        out_sems,
    )
    for copy in parent_copies + out_copies:
        copy.wait()


def send_kernel(
    me_ref, first_ref, table_hbm, out_hbm, table_ref, out_ref, picks, picks_s, sem, table_sem, sems
):
    table_copy = pltpu.make_async_copy(table_hbm, table_ref, table_sem)
    table_copy.start()
    leaves, rank_k = table_ref.shape[1:3]
    peers, tall, lanes = first_ref.shape
    half = rank_k // 2
    asked = first_ref[:, half:tall].astype(F32)
    owner, local = asked[:, 0], asked[:, 1]
    place = lax.broadcasted_iota(jnp.int32, owner.shape, 1).astype(F32)
    mine = owner == me_ref[0].astype(F32)
    key = place * leaves + local
    first = jnp.min(jnp.where(mine, key, float(lanes * leaves)), axis=1, keepdims=True)
    last = jnp.max(jnp.where(mine, key, -1.0), axis=1, keepdims=True)
    column = lax.broadcasted_iota(jnp.int32, owner.shape, 1)
    both = jnp.where(column == 0, first, jnp.where(column == 1, last, 0.0)).T[:8]
    picks[...] = both.astype(jnp.int32) & (leaves - 1)
    copy = pltpu.make_async_copy(picks, picks_s, sem)
    copy.start()
    copy.wait()

    def fill(d, carry):
        out_ref[d] = table_ref[0, picks_s[0, d]] + table_ref[1, picks_s[1, d]]
        return carry

    table_copy.wait()
    pieces = sems.shape[0]
    part = peers // pieces
    copies = []
    for i in range(pieces):
        span = slice(i * part, (i + 1) * part)
        lax.fori_loop(i * part, (i + 1) * part, fill, 0, unroll=8)
        copies.append(pltpu.make_async_copy(out_ref.at[span], out_hbm.at[span], sems.at[i]))
        copies[-1].start()
    for copy in copies:
        copy.wait()


def gift_kernel(mine_ref, sibling_ref, first_ref, own_ref, gift_ref, sems):
    slots, half = own_ref.shape[:2]

    def start(s, carry):
        for i, (source, out) in enumerate([(mine_ref, own_ref), (sibling_ref, gift_ref)]):
            pltpu.make_async_copy(
                first_ref.at[source[s] >> 1, 0:half], out.at[s], sems.at[i]
            ).start()
        return carry

    lax.fori_loop(0, slots, start, 0, unroll=8)
    for i, out in enumerate([own_ref, gift_ref]):
        pltpu.make_async_copy(first_ref.at[0:slots, 0:half], out, sems.at[i]).wait()


def inverse_kernel(base_ref, order_ref, id_ref, place_ref):
    leaves, pts = id_ref.shape
    base = base_ref[0]
    row_id = lax.broadcasted_iota(jnp.int32, (pts, pts), 0)
    tile_id = lax.broadcasted_iota(jnp.int32, (leaves, pts), 0)
    position = lax.broadcasted_iota(jnp.int32, (leaves, pts), 1).astype(F32)

    def leaf(t, total):
        local = order_rows(order_ref, base, t)
        low = local & (pts - 1)
        high = local >> log2(pts)
        onehot = jnp.where(row_id == low, 1.0, 0.0).astype(BF16)
        here = jnp.where(tile_id == high, 1.0, 0.0)
        rows = jnp.concatenate([here * t.astype(F32), here * position], axis=0)
        return total + mm(rows.astype(BF16), onehot, NT)

    total = lax.fori_loop(0, leaves, leaf, jnp.zeros((2 * leaves, pts), F32), unroll=4)
    id_ref[...] = total[0:leaves].astype(jnp.int32)
    place_ref[...] = total[leaves:].astype(jnp.int32)


def near_kernel(
    me_ref, source_ref, count_ref, left_ref, tree_ref, right_ref, out_ref,
    x_all, target_c, source_c, block_ref, weight_ref, pair_ref,
):
    leaves, height, pts = tree_ref.shape
    vectors = out_ref.shape[1]
    reach = left_ref.shape[0]
    wide = leaves + 2 * reach
    window = 2 * reach + 1
    x_all[0:reach] = left_ref[:, 0:vectors]
    x_all[reach : reach + leaves] = tree_ref[:, 0:vectors]
    x_all[reach + leaves : wide] = right_ref[:, 0:vectors]
    out_ref[...] = jnp.zeros(out_ref.shape, F32)
    lanes = source_c.shape[2] // 3
    part = lax.broadcasted_iota(jnp.int32, (ROWS, 3 * lanes), 0)
    axis_of = lax.broadcasted_iota(jnp.int32, (ROWS, 3 * lanes), 1) // lanes
    chosen = (part == axis_of) | (part == axis_of + 3) | (part == axis_of + 6)
    spread = jnp.where(chosen, float(pts), 0.0).astype(BF16)

    def prepare(ref, count, offset, own):
        def step(l, carry):
            raw = ref[l, vectors:height]
            source_c[offset + l] = mm(raw, spread, TN)
            if own:
                raw = raw.astype(F32)
                target_c[l] = (raw[0:8] + raw[3:11] + raw[6:14]) * float(pts)
            return carry

        lax.fori_loop(0, count, step, 0, unroll=2)

    prepare(left_ref, reach, 0, False)
    prepare(tree_ref, leaves, reach, True)
    prepare(right_ref, reach, reach + leaves, False)

    def tally(t, carry):
        shift = t + me_ref[0] * leaves - reach
        near, far = 0, 0
        for n in range(source_ref.shape[1]):
            m = source_ref[t, n] - shift
            live = jnp.where(count_ref[t] > n, 1, 0)
            near = near + (jnp.where(m < 8, live, 0) << (4 * (m & 7)))
            far = far + jnp.where(m < 8, 0, live)
        weight_ref[t] = near
        weight_ref[t + leaves] = far
        return carry

    lax.fori_loop(0, leaves, tally, 0, unroll=2)

    def listing(s, count):
        for m in range(window):
            t = s - m
            inside = (t >= 0) & (t < leaves)
            at = jnp.where(inside, t, 0)
            word = weight_ref[at] >> (4 * m) if m < 8 else weight_ref[at + leaves]
            weight = jnp.where(inside, word & 15, 0)
            pair_ref[count] = s + 256 * at + 65536 * weight
            count = count + jnp.where(weight > 0, 1, 0)
        pair_ref[count] = s
        return count + (count & 1)

    count = lax.fori_loop(0, wide, listing, 0)
    for i in range(2 * GROUP):
        pair_ref[count + i] = reach
    soft = delta_square * float(pts) * float(pts)

    def group(g, carry):
        for i in range(GROUP):
            n = 2 * (g * GROUP + i)
            pair = (pair_ref[n], pair_ref[n + 1])
            s = pair[0] & 255
            both = [(p >> 8) & 255 for p in pair]
            for row in range(0, pts, CHUNK):
                rows = slice(row, row + CHUNK)
                source = [source_c[s, rows, axis * lanes : (axis + 1) * lanes] for axis in range(3)]
                for h, t in enumerate(both):
                    for c in range(pts // lanes):
                        at = slice(c * lanes, (c + 1) * lanes)
                        dx, dy, dz = [target_c[t, k : k + 1, at] - source[k] for k in range(3)]
                        squared = dx * dx + dy * dy + dz * dz + soft
                        block_ref[i, rows, h * pts + c * lanes : h * pts + (c + 1) * lanes] = (
                            lax.rsqrt(squared).astype(BF16)
                        )
            product = mm(x_all[s], block_ref[i])
            for h, t in enumerate(both):
                weight = (pair[h] >> 16).astype(F32)
                out_ref[t] += weight * product[:, h * pts : (h + 1) * pts]
        return carry

    lax.fori_loop(0, (count // 2 + GROUP - 1) // GROUP, group, 0)


def top_kernel(
    me_ref, source_ref, target_ref, live_ref, coupling_ref, own_ref, other_ref, out_ref, total
):
    slots, rank_k = coupling_ref.shape[:2]
    parents, vectors = out_ref.shape[:2]
    core = me_ref[0] & (parents - 1)
    total[...] = jnp.zeros(total.shape, F32)

    def step(s, carry):
        same = (source_ref[s] & (parents - 1)) == core
        got = jnp.where(same, own_ref[s].astype(F32), other_ref[s].astype(F32))
        full = jnp.concatenate([got, pltpu.roll(got, vectors, 1)], axis=0).astype(BF16)
        term = mm(coupling_ref[s], full).astype(BF16).astype(F32)
        weight = jnp.where(live_ref[s] > 0, 1.0, 0.0)
        total[target_ref[s]] += weight * term
        return carry

    lax.fori_loop(0, slots, step, 0, unroll=8)
    for q in range(parents):
        out_ref[q] = total[q].T[:vectors].astype(BF16)


def rank_kernel(
    leaf_bits, source_ref, target_ref, live_ref, coupling_ref, word_ref, packed_ref, seen
):
    slots = source_ref.shape[0]

    def clear(i, carry):
        seen[i] = 0
        return carry

    lax.fori_loop(0, seen.shape[0], clear, 0, unroll=8)

    def rank(s, carry):
        owner = source_ref[s] >> leaf_bits
        half = jnp.where(live_ref[s] > 0, seen[owner], 2)
        word_ref[s] = owner + 256 * target_ref[s] + 65536 * half
        seen[owner] = 1
        return carry

    lax.fori_loop(0, slots, rank, 0, unroll=8)

    def pack(s, carry):
        pair = [coupling_ref[s], coupling_ref[s + slots // 2]]
        packed_ref[s] = jnp.concatenate(pair, axis=1)
        return carry

    lax.fori_loop(0, slots // 2, pack, 0, unroll=8)


def finish_kernel(
    word_ref,
    got_ref, coupling_hbm, top_hbm, transfer_hbm, basis_hbm, near_hbm, id_ref, place_ref,
    out_hbm,
    coupling_ref, top_ref, transfer_ref, basis_ref, near_ref, onehot_ref,
    total, summed, out_ref, sems, out_sems, coupling_sems,
):
    pieces = coupling_sems.shape[0]
    part = coupling_ref.shape[0] // pieces
    spans = [slice(i * part, (i + 1) * part) for i in range(pieces)]
    coupling_copies = fetch(
        [(coupling_hbm.at[span], coupling_ref.at[span]) for span in spans], coupling_sems
    )
    copies = fetch(
        [
            (top_hbm, top_ref), (transfer_hbm, transfer_ref), (basis_hbm, basis_ref),
            (near_hbm, near_ref),
        ],
        sems,
    )
    rank_k = coupling_ref.shape[1]
    leaves, vectors, pts = near_ref.shape
    total[...] = jnp.zeros(total.shape, F32)
    side = lax.broadcasted_iota(jnp.int32, (rank_k, 2 * vectors), 1) // vectors
    row_id = lax.broadcasted_iota(jnp.int32, (pts, pts), 0)
    for q in range(leaves):
        hot = jnp.where(row_id == place_ref[q : q + 1], 1.0, 0.0)
        onehot_ref[:, q * pts : (q + 1) * pts] = hot.astype(BF16)

    def step(i, carry):
        both = coupling_ref[i]
        for h in range(2):
            word = word_ref[i + h * coupling_ref.shape[0]]
            term = mm(both[:, h * rank_k : (h + 1) * rank_k], got_ref[word & 255])
            term = term.astype(BF16).astype(F32)
            total[(word >> 8) & 255] += jnp.where(side == (word >> 16), term, 0.0)
        return carry

    for span, copy in zip(spans, coupling_copies):
        copy.wait()
        lax.fori_loop(span.start, span.stop, step, 0, unroll=UNROLL)
    for copy in copies:
        copy.wait()
    for t in range(leaves):
        both = total[t]
        far = (both + pltpu.roll(both, vectors, 1)).T[:vectors]
        far = (far + mm(top_ref[t // 8], transfer_ref[t])).astype(BF16)
        value = mm(far, basis_ref[t]) + near_ref[t]
        summed[t * vectors : (t + 1) * vectors, :] = value.astype(BF16)

    out_copies = []
    for g in range(leaves // WIDE):
        leaf_id = jnp.concatenate([id_ref[g * WIDE + i : g * WIDE + i + 1] for i in range(WIDE)], axis=1)
        cols = slice(g * WIDE * pts, (g + 1) * WIDE * pts)
        spread = mm(summed[...], onehot_ref[:, cols])
        found = jnp.zeros((vectors, WIDE * pts), F32)
        for t in range(leaves):
            found = jnp.where(leaf_id == t, spread[t * vectors : (t + 1) * vectors], found)
        out_ref[:, cols] = found.astype(BF16)
        copy = pltpu.make_async_copy(out_ref.at[:, cols], out_hbm.at[:, cols], out_sems.at[g])
        copy.start()
        out_copies.append(copy)
    for copy in out_copies:
        copy.wait()


def smem():
    return pl.BlockSpec(memory_space=pltpu.SMEM)


def vmem():
    return pl.BlockSpec(memory_space=pltpu.VMEM)


def anywhere():
    return pl.BlockSpec(memory_space=pltpu.HBM)


def busy(microseconds):
    return pl.CostEstimate(
        flops=microseconds * 10**9, bytes_accessed=10**6, transcendentals=0
    )


def params(limit=SOME_VMEM):
    return pltpu.CompilerParams(vmem_limit_bytes=limit)


def shards(
    points, coords, leaf_order, leaf_basis, transfer, far_coupling, far_target, far_source,
    far_live, top_coupling, top_target, top_source, top_live, near_source, near_count,
):
    peers = lax.axis_size(AXIS)
    me = lax.axis_index(AXIS).astype(jnp.int32)
    vectors = points.shape[0]
    leaves, rank_k, pts = leaf_basis.shape
    parents = leaves // 8
    reach = leaves // 4
    height = vectors + ROWS
    slots = far_source.shape[0]
    me_s = me.reshape(1)
    base_s = me_s * (leaves * pts)
    order = leaf_order.reshape(2 * leaves, pts // 2)
    shape = jax.ShapeDtypeStruct

    tops = top_source.shape[0]
    half = rank_k // 2
    tree, head, tail, table, first = pl.pallas_call(
        tree_kernel,
        out_shape=[
            shape((leaves, height, pts), BF16),
            shape((reach, height, pts), BF16),
            shape((reach, height, pts), BF16),
            shape((2, leaves, rank_k, 2 * vectors), BF16),
            shape((peers // parents, parents, half + 8, 2 * vectors), BF16),
        ],
        in_specs=[smem()] + [anywhere()] * 5 + [vmem()] * 2,
        out_specs=[anywhere()] * 5,
        scratch_shapes=[
            pltpu.VMEM(points.shape, BF16),
            pltpu.VMEM(coords.shape, F32),
            pltpu.VMEM(order.shape, jnp.int32),
            pltpu.VMEM(leaf_basis.shape, BF16),
            pltpu.VMEM(transfer.shape, BF16),
            pltpu.VMEM((leaves * height, pts), BF16),
            pltpu.VMEM((ROWS, leaves * pts), F32),
            pltpu.VMEM((8, 2 * vectors), F32),
            pltpu.SemaphoreType.DMA((5,)),
            pltpu.VMEM((leaves, height, pts), BF16),
            pltpu.VMEM((2, leaves, rank_k, 2 * vectors), BF16),
            pltpu.VMEM((parents, REPEAT, half + 8, 2 * vectors), BF16),
            pltpu.SemaphoreType.DMA((4,)),
            pltpu.SemaphoreType.DMA((parents, peers // parents // REPEAT)),
        ],
        compiler_params=params(MOST_VMEM),
        cost_estimate=busy(7),
        name="tree",
    )(
        base_s, points, coords, order, leaf_basis, transfer,
        far_source.reshape(1, slots), top_source.reshape(1, tops),
    )
    first = first.reshape(peers, half + 8, 2 * vectors)
    first = lax.all_to_all(first, AXIS, 0, 0, tiled=True)
    ends = peers - 1
    left = lax.ppermute(tail, AXIS, [(i, i + 1) for i in range(ends)])
    right = lax.ppermute(head, AXIS, [(i + 1, i) for i in range(ends)])
    ids, places = pl.pallas_call(
        inverse_kernel,
        out_shape=[shape((leaves, pts), jnp.int32)] * 2,
        in_specs=[smem(), vmem()],
        out_specs=[vmem(), vmem()],
        compiler_params=params(),
        cost_estimate=busy(3),
        name="inverse",
    )(base_s, order)
    words, coupling = pl.pallas_call(
        functools.partial(rank_kernel, log2(leaves)),
        out_shape=[
            shape((slots,), jnp.int32),
            shape((slots // 2, rank_k, 2 * rank_k), BF16),
        ],
        in_specs=[smem()] * 3 + [vmem()],
        out_specs=[smem(), vmem()],
        scratch_shapes=[pltpu.SMEM((peers,), jnp.int32)],
        compiler_params=params(MOST_VMEM),
        cost_estimate=busy(3),
        name="rank",
    )(far_source, far_target, far_live, far_coupling)
    first, table, places, coupling, left, right = lax.optimization_barrier(
        (first, table, places, coupling, left, right)
    )
    send = pl.pallas_call(
        send_kernel,
        out_shape=shape((peers, rank_k, 2 * vectors), BF16),
        in_specs=[smem(), vmem(), anywhere()],
        out_specs=anywhere(),
        scratch_shapes=[
            pltpu.VMEM(table.shape, BF16),
            pltpu.VMEM((peers, rank_k, 2 * vectors), BF16),
            pltpu.VMEM((8, peers), jnp.int32),
            pltpu.SMEM((8, peers), jnp.int32),
            pltpu.SemaphoreType.DMA,
            pltpu.SemaphoreType.DMA,
            pltpu.SemaphoreType.DMA((4,)),
        ],
        compiler_params=params(SEND_VMEM),
        cost_estimate=busy(2),
        name="send",
    )(me_s, first, table)
    got = lax.all_to_all(send, AXIS, 0, 0, tiled=True)
    sibling = lax.dynamic_slice(first, (me ^ 1, half + 2, 0), (1, 2, tops))[0].astype(jnp.int32)
    sibling = sibling[0] * parents + sibling[1]
    block = shape((tops, half, 2 * vectors), BF16)
    own_blocks, gift = pl.pallas_call(
        gift_kernel,
        out_shape=[block, block],
        in_specs=[smem(), smem(), vmem()],
        out_specs=[vmem(), vmem()],
        scratch_shapes=[pltpu.SemaphoreType.DMA((2,))],
        compiler_params=params(),
        cost_estimate=busy(2),
        name="gift",
    )(top_source, sibling, first)
    other_blocks = lax.ppermute(gift, AXIS, [(i, i ^ 1) for i in range(peers)])
    near = pl.pallas_call(
        near_kernel,
        out_shape=shape((leaves, vectors, pts), F32),
        in_specs=[smem()] * 3 + [vmem()] * 3,
        out_specs=vmem(),
        scratch_shapes=[
            pltpu.VMEM((leaves + 2 * reach, vectors, pts), BF16),
            pltpu.VMEM((leaves, 8, pts), F32),
            pltpu.VMEM((leaves + 2 * reach, pts, 3 * 128), F32),
            pltpu.VMEM((GROUP, pts, 2 * pts), BF16),
            pltpu.SMEM((2 * leaves,), jnp.int32),
            pltpu.SMEM(((2 * reach + 2) * (leaves + 2 * reach) + 2 * GROUP + 2,), jnp.int32),
        ],
        compiler_params=params(),
        cost_estimate=busy(19),
        name="near",
    )(me_s, near_source, near_count, left, tree, right)
    top_far = pl.pallas_call(
        top_kernel,
        out_shape=shape((parents, vectors, rank_k), BF16),
        in_specs=[smem()] * 4 + [vmem()] * 3,
        out_specs=vmem(),
        scratch_shapes=[pltpu.VMEM((parents, rank_k, 2 * vectors), F32)],
        compiler_params=params(),
        cost_estimate=busy(2),
        name="top",
    )(me_s, top_source, top_target, top_live, top_coupling, own_blocks, other_blocks)
    got, near, top_far = lax.optimization_barrier((got, near, top_far))
    return pl.pallas_call(
        finish_kernel,
        out_shape=shape((vectors, leaves * pts), BF16),
        in_specs=[smem(), vmem()] + [anywhere()] * 5 + [vmem()] * 2,
        out_specs=anywhere(),
        scratch_shapes=[
            pltpu.VMEM(coupling.shape, BF16),
            pltpu.VMEM(top_far.shape, BF16),
            pltpu.VMEM(transfer.shape, BF16),
            pltpu.VMEM(leaf_basis.shape, BF16),
            pltpu.VMEM(near.shape, F32),
            pltpu.VMEM((pts, leaves * pts), BF16),
            pltpu.VMEM((leaves, rank_k, 2 * vectors), F32),
            pltpu.VMEM((leaves * vectors, pts), BF16),
            pltpu.VMEM((vectors, leaves * pts), BF16),
            pltpu.SemaphoreType.DMA((4,)),
            pltpu.SemaphoreType.DMA((leaves // WIDE,)),
            pltpu.SemaphoreType.DMA((4,)),
        ],
        compiler_params=params(LAST_VMEM),
        cost_estimate=busy(8),
        name="finish",
    )(
        words, got, coupling, top_far, transfer, leaf_basis, near, ids, places,
    )


def solution(mesh):
    placed = (
        P(None, AXIS), P(None, AXIS), P(AXIS), P(AXIS, None, None), P(AXIS, None, None),
        P(AXIS, None, None), P(AXIS), P(AXIS), P(AXIS), P(AXIS, None, None), P(AXIS), P(AXIS),
        P(AXIS), P(AXIS, None), P(AXIS),
    )
    return jax.shard_map(
        shards, mesh=mesh, in_specs=placed, out_specs=P(None, AXIS), check_vma=False
    )
```

```python
import functools

import jax
import jax.numpy as jnp
from jax import lax
from jax.experimental import pallas as pl
from jax.experimental.pallas import tpu as pltpu
from jax.sharding import PartitionSpec as P

delta_square = 0.0025
AXIS = "leaf"
ROWS = 16
GROUP = 4
WIDE = 8
CHUNK = 32
REPEAT = 16
UNROLL = 16
MOST_VMEM = 60 * 1024 * 1024
SOME_VMEM = 40 * 1024 * 1024
SEND_VMEM = SOME_VMEM
LAST_VMEM = 61 * 1024 * 1024
F32 = jnp.float32
BF16 = jnp.bfloat16

NT = (((1,), (1,)), ((), ()))
TN = (((0,), (0,)), ((), ()))


def mm(a, b, dims=(((1,), (0,)), ((), ()))):
    return lax.dot_general(a, b, dims, preferred_element_type=F32)


def log2(n):
    return n.bit_length() - 1


def three_parts(v):
    hi = v.astype(BF16).astype(F32)
    mid = (v - hi).astype(BF16).astype(F32)
    return hi, mid, (v - hi) - mid


def order_rows(order_ref, base, t, count=1):
    rows = [order_ref[pl.ds(2 * t + h, 1), :] for h in range(2 * count)]
    return jnp.concatenate(rows, axis=1) - base


def fetch(pairs, sems):
    copies = [pltpu.make_async_copy(src, dst, sems.at[i]) for i, (src, dst) in enumerate(pairs)]
    for copy in copies:
        copy.start()
    return copies


def tree_kernel(
    base_ref, points_hbm, coords_hbm, order_hbm, basis_hbm, transfer_hbm, far_ref, top_ref,
    tree_hbm, head_hbm, tail_hbm, table_hbm, first_hbm,
    points_ref, coords_ref, order_ref, basis_ref, transfer_ref, stacked, parts, extra, sems,
    tree_ref, table_ref, first_ref, out_sems, first_sem,
):
    copies = fetch(
        [
            (order_hbm, order_ref), (coords_hbm, coords_ref), (points_hbm, points_ref),
            (basis_hbm, basis_ref), (transfer_hbm, transfer_ref),
        ],
        sems,
    )
    leaves, rank_k, pts = basis_ref.shape
    vectors = points_ref.shape[0]
    height = vectors + ROWS
    reach = head_hbm.shape[0]
    base = base_ref[0]
    parts[...] = jnp.zeros(parts.shape, F32)
    for copy in copies[:3]:
        copy.wait()
    hi, mid, lo = three_parts(coords_ref[...])
    parts[0:3, :] = hi
    parts[3:6, :] = mid
    parts[6:9, :] = lo
    for q in range(leaves):
        stacked[q * height : q * height + vectors, :] = points_ref[:, q * pts : (q + 1) * pts]
        stacked[q * height + vectors : (q + 1) * height, :] = parts[
            :, q * pts : (q + 1) * pts
        ].astype(BF16)
    row_id = lax.broadcasted_iota(jnp.int32, (pts, WIDE * pts), 0)
    for copy in copies[3:]:
        copy.wait()

    def gather(g, carry):
        local = order_rows(order_ref, base, g * WIDE, WIDE)
        low = local & (pts - 1)
        high = local >> log2(pts)
        onehot = jnp.where(row_id == low, 1.0, 0.0).astype(BF16)
        spread = mm(stacked[...], onehot)
        both = jnp.zeros((height, WIDE * pts), F32)
        for q in range(leaves):
            both = jnp.where(high == q, spread[q * height : (q + 1) * height, :], both)
        both = both.astype(BF16)
        for i in range(WIDE):
            t = g * WIDE + i
            found = both[:, i * pts : (i + 1) * pts]
            tree_ref[t] = found
            twice = jnp.concatenate([found[:vectors], found[:vectors]], axis=0)
            coeff = mm(basis_ref[t], twice, NT)
            left = lax.broadcasted_iota(jnp.int32, coeff.shape, 1) < vectors
            table_ref[0, t] = jnp.where(left, coeff, 0.0).astype(BF16)
            table_ref[1, t] = jnp.where(left, 0.0, coeff).astype(BF16)
            coeff = coeff.astype(BF16)
        return carry

    half = rank_k // 2
    parents = leaves // 8
    extra[...] = jnp.zeros(extra.shape, F32)
    extra[0:1, :] = (far_ref[...] >> log2(leaves)).astype(F32)
    extra[1:2, :] = (far_ref[...] & (leaves - 1)).astype(F32)
    tops = top_ref.shape[1]
    extra[2:3, 0:tops] = (top_ref[...] >> log2(parents)).astype(F32)
    extra[3:4, 0:tops] = (top_ref[...] & (parents - 1)).astype(F32)
    repeat, couples = first_ref.shape[1], first_hbm.shape[0]
    parent_copies, out_copies = [], []
    for q in range(parents):
        for g in range(8 * q // WIDE, max(8 * (q + 1) // WIDE, 8 * q // WIDE + 1)):
            gather(g, 0)
        span = slice(8 * q, 8 * q + 8)
        pairs = [
            (table_ref.at[:, span], table_hbm.at[:, span]),
            (tree_ref.at[span], tree_hbm.at[span]),
        ]
        if q == 0:
            pairs.append((tree_ref.at[0:reach], head_hbm))
        if q == parents - 1:
            pairs.append((tree_ref.at[leaves - reach : leaves], tail_hbm))
        if q < parents - 1:
            out_copies += fetch(pairs, out_sems.at[q])
        total = jnp.zeros((rank_k, 2 * vectors), F32)
        for c in range(8 * q, 8 * q + 8):
            total = total + mm(transfer_ref[c], table_ref[0, c] + table_ref[1, c])
        left = lax.broadcasted_iota(jnp.int32, (half, 2 * vectors), 1) < vectors
        block = jnp.where(left, total[:half], total[half:])
        block = jnp.concatenate([block, extra[...]], axis=0).astype(BF16)
        for i in range(repeat):
            first_ref[q, i] = block
        parent_copies += fetch(
            [
                (first_ref.at[q], first_hbm.at[i * repeat : (i + 1) * repeat, q])
                for i in range(couples // repeat)
            ],
            first_sem.at[q],
        )
        if q == parents - 1:
            out_copies += fetch(pairs, out_sems.at[q])
    for copy in parent_copies + out_copies:
        copy.wait()


def send_kernel(
    me_ref, first_ref, table_hbm, out_hbm, table_ref, out_ref, picks, picks_s, sem, table_sem, sems
):
    table_copy = pltpu.make_async_copy(table_hbm, table_ref, table_sem)
    table_copy.start()
    leaves, rank_k = table_ref.shape[1:3]
    peers, tall, lanes = first_ref.shape
    half = rank_k // 2
    asked = first_ref[:, half:tall].astype(F32)
    owner, local = asked[:, 0], asked[:, 1]
    place = lax.broadcasted_iota(jnp.int32, owner.shape, 1).astype(F32)
    mine = owner == me_ref[0].astype(F32)
    key = place * leaves + local
    first = jnp.min(jnp.where(mine, key, float(lanes * leaves)), axis=1, keepdims=True)
    last = jnp.max(jnp.where(mine, key, -1.0), axis=1, keepdims=True)
    column = lax.broadcasted_iota(jnp.int32, owner.shape, 1)
    both = jnp.where(column == 0, first, jnp.where(column == 1, last, 0.0)).T[:8]
    picks[...] = both.astype(jnp.int32) & (leaves - 1)
    copy = pltpu.make_async_copy(picks, picks_s, sem)
    copy.start()
    copy.wait()

    def fill(d, carry):
        out_ref[d] = table_ref[0, picks_s[0, d]] + table_ref[1, picks_s[1, d]]
        return carry

    table_copy.wait()
    pieces = sems.shape[0]
    part = peers // pieces
    copies = []
    for i in range(pieces):
        span = slice(i * part, (i + 1) * part)
        lax.fori_loop(i * part, (i + 1) * part, fill, 0, unroll=8)
        copies.append(pltpu.make_async_copy(out_ref.at[span], out_hbm.at[span], sems.at[i]))
        copies[-1].start()
    for copy in copies:
        copy.wait()


def gift_kernel(mine_ref, sibling_ref, first_ref, own_ref, gift_ref, sems):
    slots, half = own_ref.shape[:2]

    def start(s, carry):
        for i, (source, out) in enumerate([(mine_ref, own_ref), (sibling_ref, gift_ref)]):
            pltpu.make_async_copy(
                first_ref.at[source[s] >> 1, 0:half], out.at[s], sems.at[i]
            ).start()
        return carry

    lax.fori_loop(0, slots, start, 0, unroll=8)
    for i, out in enumerate([own_ref, gift_ref]):
        pltpu.make_async_copy(first_ref.at[0:slots, 0:half], out, sems.at[i]).wait()


def inverse_kernel(base_ref, order_ref, id_ref, place_ref):
    leaves, pts = id_ref.shape
    base = base_ref[0]
    row_id = lax.broadcasted_iota(jnp.int32, (pts, pts), 0)
    tile_id = lax.broadcasted_iota(jnp.int32, (leaves, pts), 0)
    position = lax.broadcasted_iota(jnp.int32, (leaves, pts), 1).astype(F32)

    def leaf(t, total):
        local = order_rows(order_ref, base, t)
        low = local & (pts - 1)
        high = local >> log2(pts)
        onehot = jnp.where(row_id == low, 1.0, 0.0).astype(BF16)
        here = jnp.where(tile_id == high, 1.0, 0.0)
        rows = jnp.concatenate([here * t.astype(F32), here * position], axis=0)
        return total + mm(rows.astype(BF16), onehot, NT)

    total = lax.fori_loop(0, leaves, leaf, jnp.zeros((2 * leaves, pts), F32), unroll=4)
    id_ref[...] = total[0:leaves].astype(jnp.int32)
    place_ref[...] = total[leaves:].astype(jnp.int32)


def near_kernel(
    me_ref, source_ref, count_ref, left_ref, tree_ref, right_ref, out_ref,
    x_all, target_c, source_c, block_ref, weight_ref, pair_ref,
):
    leaves, height, pts = tree_ref.shape
    vectors = out_ref.shape[1]
    reach = left_ref.shape[0]
    wide = leaves + 2 * reach
    window = 2 * reach + 1
    x_all[0:reach] = left_ref[:, 0:vectors]
    x_all[reach : reach + leaves] = tree_ref[:, 0:vectors]
    x_all[reach + leaves : wide] = right_ref[:, 0:vectors]
    out_ref[...] = jnp.zeros(out_ref.shape, F32)
    lanes = source_c.shape[2] // 3
    part = lax.broadcasted_iota(jnp.int32, (ROWS, 3 * lanes), 0)
    axis_of = lax.broadcasted_iota(jnp.int32, (ROWS, 3 * lanes), 1) // lanes
    chosen = (part == axis_of) | (part == axis_of + 3) | (part == axis_of + 6)
    spread = jnp.where(chosen, float(pts), 0.0).astype(BF16)

    def prepare(ref, count, offset, own):
        def step(l, carry):
            raw = ref[l, vectors:height]
            source_c[offset + l] = mm(raw, spread, TN)
            if own:
                raw = raw.astype(F32)
                target_c[l] = (raw[0:8] + raw[3:11] + raw[6:14]) * float(pts)
            return carry

        lax.fori_loop(0, count, step, 0, unroll=2)

    prepare(left_ref, reach, 0, False)
    prepare(tree_ref, leaves, reach, True)
    prepare(right_ref, reach, reach + leaves, False)

    def tally(t, carry):
        shift = t + me_ref[0] * leaves - reach
        near, far = 0, 0
        for n in range(source_ref.shape[1]):
            m = source_ref[t, n] - shift
            live = jnp.where(count_ref[t] > n, 1, 0)
            near = near + (jnp.where(m < 8, live, 0) << (4 * (m & 7)))
            far = far + jnp.where(m < 8, 0, live)
        weight_ref[t] = near
        weight_ref[t + leaves] = far
        return carry

    lax.fori_loop(0, leaves, tally, 0, unroll=2)

    def listing(s, count):
        for m in range(window):
            t = s - m
            inside = (t >= 0) & (t < leaves)
            at = jnp.where(inside, t, 0)
            word = weight_ref[at] >> (4 * m) if m < 8 else weight_ref[at + leaves]
            weight = jnp.where(inside, word & 15, 0)
            pair_ref[count] = s + 256 * at + 65536 * weight
            count = count + jnp.where(weight > 0, 1, 0)
        pair_ref[count] = s
        return count + (count & 1)

    count = lax.fori_loop(0, wide, listing, 0)
    for i in range(2 * GROUP):
        pair_ref[count + i] = reach
    soft = delta_square * float(pts) * float(pts)

    def group(g, carry):
        for i in range(GROUP):
            n = 2 * (g * GROUP + i)
            pair = (pair_ref[n], pair_ref[n + 1])
            s = pair[0] & 255
            both = [(p >> 8) & 255 for p in pair]
            for row in range(0, pts, CHUNK):
                rows = slice(row, row + CHUNK)
                source = [source_c[s, rows, axis * lanes : (axis + 1) * lanes] for axis in range(3)]
                for h, t in enumerate(both):
                    for c in range(pts // lanes):
                        at = slice(c * lanes, (c + 1) * lanes)
                        dx, dy, dz = [target_c[t, k : k + 1, at] - source[k] for k in range(3)]
                        squared = dx * dx + dy * dy + dz * dz + soft
                        block_ref[i, rows, h * pts + c * lanes : h * pts + (c + 1) * lanes] = (
                            lax.rsqrt(squared).astype(BF16)
                        )
            product = mm(x_all[s], block_ref[i])
            for h, t in enumerate(both):
                weight = (pair[h] >> 16).astype(F32)
                out_ref[t] += weight * product[:, h * pts : (h + 1) * pts]
        return carry

    lax.fori_loop(0, (count // 2 + GROUP - 1) // GROUP, group, 0)


def top_kernel(
    me_ref, source_ref, target_ref, live_ref, coupling_ref, own_ref, other_ref, out_ref, total
):
    slots, rank_k = coupling_ref.shape[:2]
    parents, vectors = out_ref.shape[:2]
    core = me_ref[0] & (parents - 1)
    total[...] = jnp.zeros(total.shape, F32)

    def step(s, carry):
        same = (source_ref[s] & (parents - 1)) == core
        got = jnp.where(same, own_ref[s].astype(F32), other_ref[s].astype(F32))
        full = jnp.concatenate([got, pltpu.roll(got, vectors, 1)], axis=0).astype(BF16)
        term = mm(coupling_ref[s], full).astype(BF16).astype(F32)
        weight = jnp.where(live_ref[s] > 0, 1.0, 0.0)
        total[target_ref[s]] += weight * term
        return carry

    lax.fori_loop(0, slots, step, 0, unroll=8)
    for q in range(parents):
        out_ref[q] = total[q].T[:vectors].astype(BF16)


def rank_kernel(
    leaf_bits, source_ref, target_ref, live_ref, coupling_ref, word_ref, packed_ref, seen
):
    slots = source_ref.shape[0]

    def clear(i, carry):
        seen[i] = 0
        return carry

    lax.fori_loop(0, seen.shape[0], clear, 0, unroll=8)

    def rank(s, carry):
        owner = source_ref[s] >> leaf_bits
        half = jnp.where(live_ref[s] > 0, seen[owner], 2)
        word_ref[s] = owner + 256 * target_ref[s] + 65536 * half
        seen[owner] = 1
        return carry

    lax.fori_loop(0, slots, rank, 0, unroll=8)

    def pack(s, carry):
        pair = [coupling_ref[s], coupling_ref[s + slots // 2]]
        packed_ref[s] = jnp.concatenate(pair, axis=1)
        return carry

    lax.fori_loop(0, slots // 2, pack, 0, unroll=8)


def finish_kernel(
    word_ref,
    got_ref, coupling_hbm, top_hbm, transfer_hbm, basis_hbm, near_hbm, id_ref, place_ref,
    out_hbm,
    coupling_ref, top_ref, transfer_ref, basis_ref, near_ref, onehot_ref,
    total, summed, out_ref, sems, out_sems, coupling_sems,
):
    pieces = coupling_sems.shape[0]
    part = coupling_ref.shape[0] // pieces
    spans = [slice(i * part, (i + 1) * part) for i in range(pieces)]
    coupling_copies = fetch(
        [(coupling_hbm.at[span], coupling_ref.at[span]) for span in spans], coupling_sems
    )
    copies = fetch(
        [
            (top_hbm, top_ref), (transfer_hbm, transfer_ref), (basis_hbm, basis_ref),
            (near_hbm, near_ref),
        ],
        sems,
    )
    rank_k = coupling_ref.shape[1]
    leaves, vectors, pts = near_ref.shape
    total[...] = jnp.zeros(total.shape, F32)
    side = lax.broadcasted_iota(jnp.int32, (rank_k, 2 * vectors), 1) // vectors
    row_id = lax.broadcasted_iota(jnp.int32, (pts, pts), 0)
    for q in range(leaves):
        hot = jnp.where(row_id == place_ref[q : q + 1], 1.0, 0.0)
        onehot_ref[:, q * pts : (q + 1) * pts] = hot.astype(BF16)

    def step(i, carry):
        both = coupling_ref[i]
        for h in range(2):
            word = word_ref[i + h * coupling_ref.shape[0]]
            term = mm(both[:, h * rank_k : (h + 1) * rank_k], got_ref[word & 255])
            term = term.astype(BF16).astype(F32)
            total[(word >> 8) & 255] += jnp.where(side == (word >> 16), term, 0.0)
        return carry

    for span, copy in zip(spans, coupling_copies):
        copy.wait()
        lax.fori_loop(span.start, span.stop, step, 0, unroll=UNROLL)
    for copy in copies:
        copy.wait()
    for t in range(leaves):
        both = total[t]
        far = (both + pltpu.roll(both, vectors, 1)).T[:vectors]
        far = (far + mm(top_ref[t // 8], transfer_ref[t])).astype(BF16)
        value = mm(far, basis_ref[t]) + near_ref[t]
        summed[t * vectors : (t + 1) * vectors, :] = value.astype(BF16)

    out_copies = []
    for g in range(leaves // WIDE):
        leaf_id = jnp.concatenate([id_ref[g * WIDE + i : g * WIDE + i + 1] for i in range(WIDE)], axis=1)
        cols = slice(g * WIDE * pts, (g + 1) * WIDE * pts)
        spread = mm(summed[...], onehot_ref[:, cols])
        found = jnp.zeros((vectors, WIDE * pts), F32)
        for t in range(leaves):
            found = jnp.where(leaf_id == t, spread[t * vectors : (t + 1) * vectors], found)
        out_ref[:, cols] = found.astype(BF16)
        copy = pltpu.make_async_copy(out_ref.at[:, cols], out_hbm.at[:, cols], out_sems.at[g])
        copy.start()
        out_copies.append(copy)
    for copy in out_copies:
        copy.wait()


def smem():
    return pl.BlockSpec(memory_space=pltpu.SMEM)


def vmem():
    return pl.BlockSpec(memory_space=pltpu.VMEM)


def anywhere():
    return pl.BlockSpec(memory_space=pltpu.HBM)


def busy(microseconds):
    return pl.CostEstimate(
        flops=microseconds * 10**9, bytes_accessed=10**6, transcendentals=0
    )


def params(limit=SOME_VMEM):
    return pltpu.CompilerParams(vmem_limit_bytes=limit)


def shards(
    points, coords, leaf_order, leaf_basis, transfer, far_coupling, far_target, far_source,
    far_live, top_coupling, top_target, top_source, top_live, near_source, near_count,
):
    peers = lax.axis_size(AXIS)
    me = lax.axis_index(AXIS).astype(jnp.int32)
    vectors = points.shape[0]
    leaves, rank_k, pts = leaf_basis.shape
    parents = leaves // 8
    reach = leaves // 4
    height = vectors + ROWS
    slots = far_source.shape[0]
    me_s = me.reshape(1)
    base_s = me_s * (leaves * pts)
    order = leaf_order.reshape(2 * leaves, pts // 2)
    shape = jax.ShapeDtypeStruct

    tops = top_source.shape[0]
    half = rank_k // 2
    tree, head, tail, table, first = pl.pallas_call(
        tree_kernel,
        out_shape=[
            shape((leaves, height, pts), BF16),
            shape((reach, height, pts), BF16),
            shape((reach, height, pts), BF16),
            shape((2, leaves, rank_k, 2 * vectors), BF16),
            shape((peers // parents, parents, half + 8, 2 * vectors), BF16),
        ],
        in_specs=[smem()] + [anywhere()] * 5 + [vmem()] * 2,
        out_specs=[anywhere()] * 5,
        scratch_shapes=[
            pltpu.VMEM(points.shape, BF16),
            pltpu.VMEM(coords.shape, F32),
            pltpu.VMEM(order.shape, jnp.int32),
            pltpu.VMEM(leaf_basis.shape, BF16),
            pltpu.VMEM(transfer.shape, BF16),
            pltpu.VMEM((leaves * height, pts), BF16),
            pltpu.VMEM((ROWS, leaves * pts), F32),
            pltpu.VMEM((8, 2 * vectors), F32),
            pltpu.SemaphoreType.DMA((5,)),
            pltpu.VMEM((leaves, height, pts), BF16),
            pltpu.VMEM((2, leaves, rank_k, 2 * vectors), BF16),
            pltpu.VMEM((parents, REPEAT, half + 8, 2 * vectors), BF16),
            pltpu.SemaphoreType.DMA((parents, 4)),
            pltpu.SemaphoreType.DMA((parents, peers // parents // REPEAT)),
        ],
        compiler_params=params(MOST_VMEM),
        cost_estimate=busy(7),
        name="tree",
    )(
        base_s, points, coords, order, leaf_basis, transfer,
        far_source.reshape(1, slots), top_source.reshape(1, tops),
    )
    first = first.reshape(peers, half + 8, 2 * vectors)
    first = lax.all_to_all(first, AXIS, 0, 0, tiled=True)
    ends = peers - 1
    left = lax.ppermute(tail, AXIS, [(i, i + 1) for i in range(ends)])
    right = lax.ppermute(head, AXIS, [(i + 1, i) for i in range(ends)])
    ids, places = pl.pallas_call(
        inverse_kernel,
        out_shape=[shape((leaves, pts), jnp.int32)] * 2,
        in_specs=[smem(), vmem()],
        out_specs=[vmem(), vmem()],
        compiler_params=params(),
        cost_estimate=busy(3),
        name="inverse",
    )(base_s, order)
    words, coupling = pl.pallas_call(
        functools.partial(rank_kernel, log2(leaves)),
        out_shape=[
            shape((slots,), jnp.int32),
            shape((slots // 2, rank_k, 2 * rank_k), BF16),
        ],
        in_specs=[smem()] * 3 + [vmem()],
        out_specs=[smem(), vmem()],
        scratch_shapes=[pltpu.SMEM((peers,), jnp.int32)],
        compiler_params=params(MOST_VMEM),
        cost_estimate=busy(3),
        name="rank",
    )(far_source, far_target, far_live, far_coupling)
    first, table, places, coupling, left, right = lax.optimization_barrier(
        (first, table, places, coupling, left, right)
    )
    send = pl.pallas_call(
        send_kernel,
        out_shape=shape((peers, rank_k, 2 * vectors), BF16),
        in_specs=[smem(), vmem(), anywhere()],
        out_specs=anywhere(),
        scratch_shapes=[
            pltpu.VMEM(table.shape, BF16),
            pltpu.VMEM((peers, rank_k, 2 * vectors), BF16),
            pltpu.VMEM((8, peers), jnp.int32),
            pltpu.SMEM((8, peers), jnp.int32),
            pltpu.SemaphoreType.DMA,
            pltpu.SemaphoreType.DMA,
            pltpu.SemaphoreType.DMA((4,)),
        ],
        compiler_params=params(SEND_VMEM),
        cost_estimate=busy(2),
        name="send",
    )(me_s, first, table)
    got = lax.all_to_all(send, AXIS, 0, 0, tiled=True)
    sibling = lax.dynamic_slice(first, (me ^ 1, half + 2, 0), (1, 2, tops))[0].astype(jnp.int32)
    sibling = sibling[0] * parents + sibling[1]
    block = shape((tops, half, 2 * vectors), BF16)
    own_blocks, gift = pl.pallas_call(
        gift_kernel,
        out_shape=[block, block],
        in_specs=[smem(), smem(), vmem()],
        out_specs=[vmem(), vmem()],
        scratch_shapes=[pltpu.SemaphoreType.DMA((2,))],
        compiler_params=params(),
        cost_estimate=busy(2),
        name="gift",
    )(top_source, sibling, first)
    other_blocks = lax.ppermute(gift, AXIS, [(i, i ^ 1) for i in range(peers)])
    near = pl.pallas_call(
        near_kernel,
        out_shape=shape((leaves, vectors, pts), F32),
        in_specs=[smem()] * 3 + [vmem()] * 3,
        out_specs=vmem(),
        scratch_shapes=[
            pltpu.VMEM((leaves + 2 * reach, vectors, pts), BF16),
            pltpu.VMEM((leaves, 8, pts), F32),
            pltpu.VMEM((leaves + 2 * reach, pts, 3 * 128), F32),
            pltpu.VMEM((GROUP, pts, 2 * pts), BF16),
            pltpu.SMEM((2 * leaves,), jnp.int32),
            pltpu.SMEM(((2 * reach + 2) * (leaves + 2 * reach) + 2 * GROUP + 2,), jnp.int32),
        ],
        compiler_params=params(),
        cost_estimate=busy(19),
        name="near",
    )(me_s, near_source, near_count, left, tree, right)
    top_far = pl.pallas_call(
        top_kernel,
        out_shape=shape((parents, vectors, rank_k), BF16),
        in_specs=[smem()] * 4 + [vmem()] * 3,
        out_specs=vmem(),
        scratch_shapes=[pltpu.VMEM((parents, rank_k, 2 * vectors), F32)],
        compiler_params=params(),
        cost_estimate=busy(2),
        name="top",
    )(me_s, top_source, top_target, top_live, top_coupling, own_blocks, other_blocks)
    got, near, top_far = lax.optimization_barrier((got, near, top_far))
    return pl.pallas_call(
        finish_kernel,
        out_shape=shape((vectors, leaves * pts), BF16),
        in_specs=[smem(), vmem()] + [anywhere()] * 5 + [vmem()] * 2,
        out_specs=anywhere(),
        scratch_shapes=[
            pltpu.VMEM(coupling.shape, BF16),
            pltpu.VMEM(top_far.shape, BF16),
            pltpu.VMEM(transfer.shape, BF16),
            pltpu.VMEM(leaf_basis.shape, BF16),
            pltpu.VMEM(near.shape, F32),
            pltpu.VMEM((pts, leaves * pts), BF16),
            pltpu.VMEM((leaves, rank_k, 2 * vectors), F32),
            pltpu.VMEM((leaves * vectors, pts), BF16),
            pltpu.VMEM((vectors, leaves * pts), BF16),
            pltpu.SemaphoreType.DMA((4,)),
            pltpu.SemaphoreType.DMA((leaves // WIDE,)),
            pltpu.SemaphoreType.DMA((4,)),
        ],
        compiler_params=params(LAST_VMEM),
        cost_estimate=busy(8),
        name="finish",
    )(
        words, got, coupling, top_far, transfer, leaf_basis, near, ids, places,
    )


def solution(mesh):
    placed = (
        P(None, AXIS), P(None, AXIS), P(AXIS), P(AXIS, None, None), P(AXIS, None, None),
        P(AXIS, None, None), P(AXIS), P(AXIS), P(AXIS), P(AXIS, None, None), P(AXIS), P(AXIS),
        P(AXIS), P(AXIS, None), P(AXIS),
    )
    return jax.shard_map(
        shards, mesh=mesh, in_specs=placed, out_specs=P(None, AXIS), check_vma=False
    )
```

```python
import functools

import jax
import jax.numpy as jnp
from jax import lax
from jax.experimental import pallas as pl
from jax.experimental.pallas import tpu as pltpu
from jax.sharding import PartitionSpec as P

delta_square = 0.0025
AXIS = "leaf"
ROWS = 16
GROUP = 4
WIDE = 8
CHUNK = 32
REPEAT = 16
UNROLL = 16
GOT = 4
MOST_VMEM = 60 * 1024 * 1024
SOME_VMEM = 40 * 1024 * 1024
SEND_VMEM = SOME_VMEM
LAST_VMEM = 61 * 1024 * 1024
F32 = jnp.float32
BF16 = jnp.bfloat16

NT = (((1,), (1,)), ((), ()))
TN = (((0,), (0,)), ((), ()))


def mm(a, b, dims=(((1,), (0,)), ((), ()))):
    return lax.dot_general(a, b, dims, preferred_element_type=F32)


def log2(n):
    return n.bit_length() - 1


def three_parts(v):
    hi = v.astype(BF16).astype(F32)
    mid = (v - hi).astype(BF16).astype(F32)
    return hi, mid, (v - hi) - mid


def order_rows(order_ref, base, t, count=1):
    rows = [order_ref[pl.ds(2 * t + h, 1), :] for h in range(2 * count)]
    return jnp.concatenate(rows, axis=1) - base


def fetch(pairs, sems):
    copies = [pltpu.make_async_copy(src, dst, sems.at[i]) for i, (src, dst) in enumerate(pairs)]
    for copy in copies:
        copy.start()
    return copies


def tree_kernel(
    base_ref, points_hbm, coords_hbm, order_hbm, basis_hbm, transfer_hbm, far_ref, top_ref,
    tree_hbm, head_hbm, tail_hbm, table_hbm, first_hbm,
    points_ref, coords_ref, order_ref, basis_ref, transfer_ref, stacked, parts, extra, sems,
    tree_ref, table_ref, first_ref, out_sems, first_sem,
):
    copies = fetch(
        [
            (order_hbm, order_ref), (coords_hbm, coords_ref), (points_hbm, points_ref),
            (basis_hbm, basis_ref), (transfer_hbm, transfer_ref),
        ],
        sems,
    )
    leaves, rank_k, pts = basis_ref.shape
    vectors = points_ref.shape[0]
    height = vectors + ROWS
    reach = head_hbm.shape[0]
    base = base_ref[0]
    parts[...] = jnp.zeros(parts.shape, F32)
    for copy in copies[:3]:
        copy.wait()
    hi, mid, lo = three_parts(coords_ref[...])
    parts[0:3, :] = hi
    parts[3:6, :] = mid
    parts[6:9, :] = lo
    for q in range(leaves):
        stacked[q * height : q * height + vectors, :] = points_ref[:, q * pts : (q + 1) * pts]
        stacked[q * height + vectors : (q + 1) * height, :] = parts[
            :, q * pts : (q + 1) * pts
        ].astype(BF16)
    row_id = lax.broadcasted_iota(jnp.int32, (pts, WIDE * pts), 0)
    for copy in copies[3:]:
        copy.wait()

    def gather(g, carry):
        local = order_rows(order_ref, base, g * WIDE, WIDE)
        low = local & (pts - 1)
        high = local >> log2(pts)
        onehot = jnp.where(row_id == low, 1.0, 0.0).astype(BF16)
        spread = mm(stacked[...], onehot)
        both = jnp.zeros((height, WIDE * pts), F32)
        for q in range(leaves):
            both = jnp.where(high == q, spread[q * height : (q + 1) * height, :], both)
        both = both.astype(BF16)
        for i in range(WIDE):
            t = g * WIDE + i
            found = both[:, i * pts : (i + 1) * pts]
            tree_ref[t] = found
            twice = jnp.concatenate([found[:vectors], found[:vectors]], axis=0)
            coeff = mm(basis_ref[t], twice, NT)
            left = lax.broadcasted_iota(jnp.int32, coeff.shape, 1) < vectors
            table_ref[0, t] = jnp.where(left, coeff, 0.0).astype(BF16)
            table_ref[1, t] = jnp.where(left, 0.0, coeff).astype(BF16)
            coeff = coeff.astype(BF16)
        return carry

    half = rank_k // 2
    parents = leaves // 8
    extra[...] = jnp.zeros(extra.shape, F32)
    extra[0:1, :] = (far_ref[...] >> log2(leaves)).astype(F32)
    extra[1:2, :] = (far_ref[...] & (leaves - 1)).astype(F32)
    tops = top_ref.shape[1]
    extra[2:3, 0:tops] = (top_ref[...] >> log2(parents)).astype(F32)
    extra[3:4, 0:tops] = (top_ref[...] & (parents - 1)).astype(F32)
    repeat, couples = first_ref.shape[1], first_hbm.shape[0]
    parent_copies, out_copies = [], []
    for q in range(parents):
        for g in range(8 * q // WIDE, max(8 * (q + 1) // WIDE, 8 * q // WIDE + 1)):
            gather(g, 0)
        span = slice(8 * q, 8 * q + 8)
        pairs = [
            (table_ref.at[:, span], table_hbm.at[:, span]),
            (tree_ref.at[span], tree_hbm.at[span]),
        ]
        if q == 0:
            pairs.append((tree_ref.at[0:reach], head_hbm))
        if q == parents - 1:
            pairs.append((tree_ref.at[leaves - reach : leaves], tail_hbm))
        if q < parents - 1:
            out_copies += fetch(pairs, out_sems.at[q])
        total = jnp.zeros((rank_k, 2 * vectors), F32)
        for c in range(8 * q, 8 * q + 8):
            total = total + mm(transfer_ref[c], table_ref[0, c] + table_ref[1, c])
        left = lax.broadcasted_iota(jnp.int32, (half, 2 * vectors), 1) < vectors
        block = jnp.where(left, total[:half], total[half:])
        block = jnp.concatenate([block, extra[...]], axis=0).astype(BF16)
        for i in range(repeat):
            first_ref[q, i] = block
        parent_copies += fetch(
            [
                (first_ref.at[q], first_hbm.at[i * repeat : (i + 1) * repeat, q])
                for i in range(couples // repeat)
            ],
            first_sem.at[q],
        )
        if q == parents - 1:
            out_copies += fetch(pairs, out_sems.at[q])
    for copy in parent_copies + out_copies:
        copy.wait()


def send_kernel(
    me_ref, first_ref, table_hbm, out_hbm, table_ref, out_ref, picks, picks_s, sem, table_sem, sems
):
    table_copy = pltpu.make_async_copy(table_hbm, table_ref, table_sem)
    table_copy.start()
    leaves, rank_k = table_ref.shape[1:3]
    peers, tall, lanes = first_ref.shape
    half = rank_k // 2
    asked = first_ref[:, half:tall].astype(F32)
    owner, local = asked[:, 0], asked[:, 1]
    place = lax.broadcasted_iota(jnp.int32, owner.shape, 1).astype(F32)
    mine = owner == me_ref[0].astype(F32)
    key = place * leaves + local
    first = jnp.min(jnp.where(mine, key, float(lanes * leaves)), axis=1, keepdims=True)
    last = jnp.max(jnp.where(mine, key, -1.0), axis=1, keepdims=True)
    column = lax.broadcasted_iota(jnp.int32, owner.shape, 1)
    both = jnp.where(column == 0, first, jnp.where(column == 1, last, 0.0)).T[:8]
    picks[...] = both.astype(jnp.int32) & (leaves - 1)
    copy = pltpu.make_async_copy(picks, picks_s, sem)
    copy.start()
    copy.wait()

    def fill(d, carry):
        out_ref[d] = table_ref[0, picks_s[0, d]] + table_ref[1, picks_s[1, d]]
        return carry

    table_copy.wait()
    pieces = sems.shape[0]
    part = peers // pieces
    copies = []
    for i in range(pieces):
        span = slice(i * part, (i + 1) * part)
        lax.fori_loop(i * part, (i + 1) * part, fill, 0, unroll=8)
        copies.append(pltpu.make_async_copy(out_ref.at[span], out_hbm.at[span], sems.at[i]))
        copies[-1].start()
    for copy in copies:
        copy.wait()


def gift_kernel(mine_ref, sibling_ref, first_ref, own_ref, gift_ref, sems):
    slots, half = own_ref.shape[:2]

    def start(s, carry):
        for i, (source, out) in enumerate([(mine_ref, own_ref), (sibling_ref, gift_ref)]):
            pltpu.make_async_copy(
                first_ref.at[source[s] >> 1, 0:half], out.at[s], sems.at[i]
            ).start()
        return carry

    lax.fori_loop(0, slots, start, 0, unroll=8)
    for i, out in enumerate([own_ref, gift_ref]):
        pltpu.make_async_copy(first_ref.at[0:slots, 0:half], out, sems.at[i]).wait()


def inverse_kernel(base_ref, order_ref, id_ref, place_ref):
    leaves, pts = id_ref.shape
    base = base_ref[0]
    row_id = lax.broadcasted_iota(jnp.int32, (pts, pts), 0)
    tile_id = lax.broadcasted_iota(jnp.int32, (leaves, pts), 0)
    position = lax.broadcasted_iota(jnp.int32, (leaves, pts), 1).astype(F32)

    def leaf(t, total):
        local = order_rows(order_ref, base, t)
        low = local & (pts - 1)
        high = local >> log2(pts)
        onehot = jnp.where(row_id == low, 1.0, 0.0).astype(BF16)
        here = jnp.where(tile_id == high, 1.0, 0.0)
        rows = jnp.concatenate([here * t.astype(F32), here * position], axis=0)
        return total + mm(rows.astype(BF16), onehot, NT)

    total = lax.fori_loop(0, leaves, leaf, jnp.zeros((2 * leaves, pts), F32), unroll=4)
    id_ref[...] = total[0:leaves].astype(jnp.int32)
    place_ref[...] = total[leaves:].astype(jnp.int32)


def near_kernel(
    me_ref, source_ref, count_ref, left_ref, tree_ref, right_ref, out_ref,
    x_all, target_c, source_c, block_ref, weight_ref, pair_ref,
):
    leaves, height, pts = tree_ref.shape
    vectors = out_ref.shape[1]
    reach = left_ref.shape[0]
    wide = leaves + 2 * reach
    window = 2 * reach + 1
    x_all[0:reach] = left_ref[:, 0:vectors]
    x_all[reach : reach + leaves] = tree_ref[:, 0:vectors]
    x_all[reach + leaves : wide] = right_ref[:, 0:vectors]
    out_ref[...] = jnp.zeros(out_ref.shape, F32)
    lanes = source_c.shape[2] // 3
    part = lax.broadcasted_iota(jnp.int32, (ROWS, 3 * lanes), 0)
    axis_of = lax.broadcasted_iota(jnp.int32, (ROWS, 3 * lanes), 1) // lanes
    chosen = (part == axis_of) | (part == axis_of + 3) | (part == axis_of + 6)
    spread = jnp.where(chosen, float(pts), 0.0).astype(BF16)

    def prepare(ref, count, offset, own):
        def step(l, carry):
            raw = ref[l, vectors:height]
            source_c[offset + l] = mm(raw, spread, TN)
            if own:
                raw = raw.astype(F32)
                target_c[l] = (raw[0:8] + raw[3:11] + raw[6:14]) * float(pts)
            return carry

        lax.fori_loop(0, count, step, 0, unroll=2)

    prepare(left_ref, reach, 0, False)
    prepare(tree_ref, leaves, reach, True)
    prepare(right_ref, reach, reach + leaves, False)

    def tally(t, carry):
        shift = t + me_ref[0] * leaves - reach
        near, far = 0, 0
        for n in range(source_ref.shape[1]):
            m = source_ref[t, n] - shift
            live = jnp.where(count_ref[t] > n, 1, 0)
            near = near + (jnp.where(m < 8, live, 0) << (4 * (m & 7)))
            far = far + jnp.where(m < 8, 0, live)
        weight_ref[t] = near
        weight_ref[t + leaves] = far
        return carry

    lax.fori_loop(0, leaves, tally, 0, unroll=2)

    def listing(s, count):
        for m in range(window):
            t = s - m
            inside = (t >= 0) & (t < leaves)
            at = jnp.where(inside, t, 0)
            word = weight_ref[at] >> (4 * m) if m < 8 else weight_ref[at + leaves]
            weight = jnp.where(inside, word & 15, 0)
            pair_ref[count] = s + 256 * at + 65536 * weight
            count = count + jnp.where(weight > 0, 1, 0)
        pair_ref[count] = s
        return count + (count & 1)

    count = lax.fori_loop(0, wide, listing, 0)
    for i in range(2 * GROUP):
        pair_ref[count + i] = reach
    soft = delta_square * float(pts) * float(pts)

    def group(g, carry):
        for i in range(GROUP):
            n = 2 * (g * GROUP + i)
            pair = (pair_ref[n], pair_ref[n + 1])
            s = pair[0] & 255
            both = [(p >> 8) & 255 for p in pair]
            for row in range(0, pts, CHUNK):
                rows = slice(row, row + CHUNK)
                source = [source_c[s, rows, axis * lanes : (axis + 1) * lanes] for axis in range(3)]
                for h, t in enumerate(both):
                    for c in range(pts // lanes):
                        at = slice(c * lanes, (c + 1) * lanes)
                        dx, dy, dz = [target_c[t, k : k + 1, at] - source[k] for k in range(3)]
                        squared = dx * dx + dy * dy + dz * dz + soft
                        block_ref[i, rows, h * pts + c * lanes : h * pts + (c + 1) * lanes] = (
                            lax.rsqrt(squared).astype(BF16)
                        )
            product = mm(x_all[s], block_ref[i])
            for h, t in enumerate(both):
                weight = (pair[h] >> 16).astype(F32)
                out_ref[t] += weight * product[:, h * pts : (h + 1) * pts]
        return carry

    lax.fori_loop(0, (count // 2 + GROUP - 1) // GROUP, group, 0)


def top_kernel(
    me_ref, source_ref, target_ref, live_ref, coupling_ref, own_ref, other_ref, out_ref, total
):
    slots, rank_k = coupling_ref.shape[:2]
    parents, vectors = out_ref.shape[:2]
    core = me_ref[0] & (parents - 1)
    total[...] = jnp.zeros(total.shape, F32)

    def step(s, carry):
        same = (source_ref[s] & (parents - 1)) == core
        got = jnp.where(same, own_ref[s].astype(F32), other_ref[s].astype(F32))
        full = jnp.concatenate([got, pltpu.roll(got, vectors, 1)], axis=0).astype(BF16)
        term = mm(coupling_ref[s], full).astype(BF16).astype(F32)
        weight = jnp.where(live_ref[s] > 0, 1.0, 0.0)
        total[target_ref[s]] += weight * term
        return carry

    lax.fori_loop(0, slots, step, 0, unroll=8)
    for q in range(parents):
        out_ref[q] = total[q].T[:vectors].astype(BF16)


def rank_kernel(
    leaf_bits, source_ref, target_ref, live_ref, coupling_ref, word_ref, packed_ref, seen
):
    slots = source_ref.shape[0]

    def clear(i, carry):
        seen[i] = 0
        return carry

    lax.fori_loop(0, seen.shape[0], clear, 0, unroll=8)

    def rank(s, carry):
        owner = source_ref[s] >> leaf_bits
        half = jnp.where(live_ref[s] > 0, seen[owner], 2)
        word_ref[s] = owner + 256 * target_ref[s] + 65536 * half
        seen[owner] = 1
        return carry

    lax.fori_loop(0, slots, rank, 0, unroll=8)

    def pack(s, carry):
        pair = [coupling_ref[s], coupling_ref[s + slots // 2]]
        packed_ref[s] = jnp.concatenate(pair, axis=1)
        return carry

    lax.fori_loop(0, slots // 2, pack, 0, unroll=8)


def finish_kernel(
    word_ref,
    got_hbm, coupling_hbm, top_hbm, transfer_hbm, basis_hbm, near_hbm, id_ref, place_ref,
    out_hbm,
    got_ref, coupling_ref, top_ref, transfer_ref, basis_ref, near_ref, onehot_ref,
    total, summed, out_ref, sems, out_sems, coupling_sems, got_sems,
):
    batch = got_ref.shape[0] // got_sems.shape[0]
    shares = [slice(i * batch, (i + 1) * batch) for i in range(got_sems.shape[0])]
    got_copies = fetch([(got_hbm.at[share], got_ref.at[share]) for share in shares], got_sems)
    pieces = coupling_sems.shape[0]
    part = coupling_ref.shape[0] // pieces
    spans = [slice(i * part, (i + 1) * part) for i in range(pieces)]
    coupling_copies = fetch(
        [(coupling_hbm.at[span], coupling_ref.at[span]) for span in spans], coupling_sems
    )
    copies = fetch(
        [
            (top_hbm, top_ref), (transfer_hbm, transfer_ref), (basis_hbm, basis_ref),
            (near_hbm, near_ref),
        ],
        sems,
    )
    rank_k = coupling_ref.shape[1]
    leaves, vectors, pts = near_ref.shape
    total[...] = jnp.zeros(total.shape, F32)
    side = lax.broadcasted_iota(jnp.int32, (rank_k, 2 * vectors), 1) // vectors
    row_id = lax.broadcasted_iota(jnp.int32, (pts, pts), 0)
    for q in range(leaves):
        hot = jnp.where(row_id == place_ref[q : q + 1], 1.0, 0.0)
        onehot_ref[:, q * pts : (q + 1) * pts] = hot.astype(BF16)

    def step(i, carry):
        both = coupling_ref[i]
        for h in range(2):
            word = word_ref[i + h * coupling_ref.shape[0]]
            term = mm(both[:, h * rank_k : (h + 1) * rank_k], got_ref[word & 255])
            term = term.astype(BF16).astype(F32)
            total[(word >> 8) & 255] += jnp.where(side == (word >> 16), term, 0.0)
        return carry

    for copy in got_copies:
        copy.wait()
    for span, copy in zip(spans, coupling_copies):
        copy.wait()
        lax.fori_loop(span.start, span.stop, step, 0, unroll=UNROLL)
    for copy in copies:
        copy.wait()
    for t in range(leaves):
        both = total[t]
        far = (both + pltpu.roll(both, vectors, 1)).T[:vectors]
        far = (far + mm(top_ref[t // 8], transfer_ref[t])).astype(BF16)
        value = mm(far, basis_ref[t]) + near_ref[t]
        summed[t * vectors : (t + 1) * vectors, :] = value.astype(BF16)

    out_copies = []
    for g in range(leaves // WIDE):
        leaf_id = jnp.concatenate([id_ref[g * WIDE + i : g * WIDE + i + 1] for i in range(WIDE)], axis=1)
        cols = slice(g * WIDE * pts, (g + 1) * WIDE * pts)
        spread = mm(summed[...], onehot_ref[:, cols])
        found = jnp.zeros((vectors, WIDE * pts), F32)
        for t in range(leaves):
            found = jnp.where(leaf_id == t, spread[t * vectors : (t + 1) * vectors], found)
        out_ref[:, cols] = found.astype(BF16)
        copy = pltpu.make_async_copy(out_ref.at[:, cols], out_hbm.at[:, cols], out_sems.at[g])
        copy.start()
        out_copies.append(copy)
    for copy in out_copies:
        copy.wait()


def smem():
    return pl.BlockSpec(memory_space=pltpu.SMEM)


def vmem():
    return pl.BlockSpec(memory_space=pltpu.VMEM)


def anywhere():
    return pl.BlockSpec(memory_space=pltpu.HBM)


def busy(microseconds):
    return pl.CostEstimate(
        flops=microseconds * 10**9, bytes_accessed=10**6, transcendentals=0
    )


def params(limit=SOME_VMEM):
    return pltpu.CompilerParams(vmem_limit_bytes=limit)


def shards(
    points, coords, leaf_order, leaf_basis, transfer, far_coupling, far_target, far_source,
    far_live, top_coupling, top_target, top_source, top_live, near_source, near_count,
):
    peers = lax.axis_size(AXIS)
    me = lax.axis_index(AXIS).astype(jnp.int32)
    vectors = points.shape[0]
    leaves, rank_k, pts = leaf_basis.shape
    parents = leaves // 8
    reach = leaves // 4
    height = vectors + ROWS
    slots = far_source.shape[0]
    me_s = me.reshape(1)
    base_s = me_s * (leaves * pts)
    order = leaf_order.reshape(2 * leaves, pts // 2)
    shape = jax.ShapeDtypeStruct

    tops = top_source.shape[0]
    half = rank_k // 2
    tree, head, tail, table, first = pl.pallas_call(
        tree_kernel,
        out_shape=[
            shape((leaves, height, pts), BF16),
            shape((reach, height, pts), BF16),
            shape((reach, height, pts), BF16),
            shape((2, leaves, rank_k, 2 * vectors), BF16),
            shape((peers // parents, parents, half + 8, 2 * vectors), BF16),
        ],
        in_specs=[smem()] + [anywhere()] * 5 + [vmem()] * 2,
        out_specs=[anywhere()] * 5,
        scratch_shapes=[
            pltpu.VMEM(points.shape, BF16),
            pltpu.VMEM(coords.shape, F32),
            pltpu.VMEM(order.shape, jnp.int32),
            pltpu.VMEM(leaf_basis.shape, BF16),
            pltpu.VMEM(transfer.shape, BF16),
            pltpu.VMEM((leaves * height, pts), BF16),
            pltpu.VMEM((ROWS, leaves * pts), F32),
            pltpu.VMEM((8, 2 * vectors), F32),
            pltpu.SemaphoreType.DMA((5,)),
            pltpu.VMEM((leaves, height, pts), BF16),
            pltpu.VMEM((2, leaves, rank_k, 2 * vectors), BF16),
            pltpu.VMEM((parents, REPEAT, half + 8, 2 * vectors), BF16),
            pltpu.SemaphoreType.DMA((parents, 4)),
            pltpu.SemaphoreType.DMA((parents, peers // parents // REPEAT)),
        ],
        compiler_params=params(MOST_VMEM),
        cost_estimate=busy(7),
        name="tree",
    )(
        base_s, points, coords, order, leaf_basis, transfer,
        far_source.reshape(1, slots), top_source.reshape(1, tops),
    )
    first = first.reshape(peers, half + 8, 2 * vectors)
    first = lax.all_to_all(first, AXIS, 0, 0, tiled=True)
    ends = peers - 1
    left = lax.ppermute(tail, AXIS, [(i, i + 1) for i in range(ends)])
    right = lax.ppermute(head, AXIS, [(i + 1, i) for i in range(ends)])
    ids, places = pl.pallas_call(
        inverse_kernel,
        out_shape=[shape((leaves, pts), jnp.int32)] * 2,
        in_specs=[smem(), vmem()],
        out_specs=[vmem(), vmem()],
        compiler_params=params(),
        cost_estimate=busy(3),
        name="inverse",
    )(base_s, order)
    words, coupling = pl.pallas_call(
        functools.partial(rank_kernel, log2(leaves)),
        out_shape=[
            shape((slots,), jnp.int32),
            shape((slots // 2, rank_k, 2 * rank_k), BF16),
        ],
        in_specs=[smem()] * 3 + [vmem()],
        out_specs=[smem(), vmem()],
        scratch_shapes=[pltpu.SMEM((peers,), jnp.int32)],
        compiler_params=params(MOST_VMEM),
        cost_estimate=busy(3),
        name="rank",
    )(far_source, far_target, far_live, far_coupling)
    first, table, places, coupling, left, right = lax.optimization_barrier(
        (first, table, places, coupling, left, right)
    )
    send = pl.pallas_call(
        send_kernel,
        out_shape=shape((peers, rank_k, 2 * vectors), BF16),
        in_specs=[smem(), vmem(), anywhere()],
        out_specs=anywhere(),
        scratch_shapes=[
            pltpu.VMEM(table.shape, BF16),
            pltpu.VMEM((peers, rank_k, 2 * vectors), BF16),
            pltpu.VMEM((8, peers), jnp.int32),
            pltpu.SMEM((8, peers), jnp.int32),
            pltpu.SemaphoreType.DMA,
            pltpu.SemaphoreType.DMA,
            pltpu.SemaphoreType.DMA((4,)),
        ],
        compiler_params=params(SEND_VMEM),
        cost_estimate=busy(2),
        name="send",
    )(me_s, first, table)
    got = lax.all_to_all(send, AXIS, 0, 0, tiled=True)
    sibling = lax.dynamic_slice(first, (me ^ 1, half + 2, 0), (1, 2, tops))[0].astype(jnp.int32)
    sibling = sibling[0] * parents + sibling[1]
    block = shape((tops, half, 2 * vectors), BF16)
    own_blocks, gift = pl.pallas_call(
        gift_kernel,
        out_shape=[block, block],
        in_specs=[smem(), smem(), vmem()],
        out_specs=[vmem(), vmem()],
        scratch_shapes=[pltpu.SemaphoreType.DMA((2,))],
        compiler_params=params(),
        cost_estimate=busy(2),
        name="gift",
    )(top_source, sibling, first)
    other_blocks = lax.ppermute(gift, AXIS, [(i, i ^ 1) for i in range(peers)])
    near = pl.pallas_call(
        near_kernel,
        out_shape=shape((leaves, vectors, pts), F32),
        in_specs=[smem()] * 3 + [vmem()] * 3,
        out_specs=vmem(),
        scratch_shapes=[
            pltpu.VMEM((leaves + 2 * reach, vectors, pts), BF16),
            pltpu.VMEM((leaves, 8, pts), F32),
            pltpu.VMEM((leaves + 2 * reach, pts, 3 * 128), F32),
            pltpu.VMEM((GROUP, pts, 2 * pts), BF16),
            pltpu.SMEM((2 * leaves,), jnp.int32),
            pltpu.SMEM(((2 * reach + 2) * (leaves + 2 * reach) + 2 * GROUP + 2,), jnp.int32),
        ],
        compiler_params=params(),
        cost_estimate=busy(19),
        name="near",
    )(me_s, near_source, near_count, left, tree, right)
    top_far = pl.pallas_call(
        top_kernel,
        out_shape=shape((parents, vectors, rank_k), BF16),
        in_specs=[smem()] * 4 + [vmem()] * 3,
        out_specs=vmem(),
        scratch_shapes=[pltpu.VMEM((parents, rank_k, 2 * vectors), F32)],
        compiler_params=params(),
        cost_estimate=busy(2),
        name="top",
    )(me_s, top_source, top_target, top_live, top_coupling, own_blocks, other_blocks)
    got, near, top_far = lax.optimization_barrier((got, near, top_far))
    return pl.pallas_call(
        finish_kernel,
        out_shape=shape((vectors, leaves * pts), BF16),
        in_specs=[smem()] + [anywhere()] * 6 + [vmem()] * 2,
        out_specs=anywhere(),
        scratch_shapes=[
            pltpu.VMEM(got.shape, BF16),
            pltpu.VMEM(coupling.shape, BF16),
            pltpu.VMEM(top_far.shape, BF16),
            pltpu.VMEM(transfer.shape, BF16),
            pltpu.VMEM(leaf_basis.shape, BF16),
            pltpu.VMEM(near.shape, F32),
            pltpu.VMEM((pts, leaves * pts), BF16),
            pltpu.VMEM((leaves, rank_k, 2 * vectors), F32),
            pltpu.VMEM((leaves * vectors, pts), BF16),
            pltpu.VMEM((vectors, leaves * pts), BF16),
            pltpu.SemaphoreType.DMA((4,)),
            pltpu.SemaphoreType.DMA((leaves // WIDE,)),
            pltpu.SemaphoreType.DMA((4,)),
            pltpu.SemaphoreType.DMA((GOT,)),
        ],
        compiler_params=params(LAST_VMEM),
        cost_estimate=busy(8),
        name="finish",
    )(
        words, got, coupling, top_far, transfer, leaf_basis, near, ids, places,
    )


def solution(mesh):
    placed = (
        P(None, AXIS), P(None, AXIS), P(AXIS), P(AXIS, None, None), P(AXIS, None, None),
        P(AXIS, None, None), P(AXIS), P(AXIS), P(AXIS), P(AXIS, None, None), P(AXIS), P(AXIS),
        P(AXIS), P(AXIS, None), P(AXIS),
    )
    return jax.shard_map(
        shards, mesh=mesh, in_specs=placed, out_specs=P(None, AXIS), check_vma=False
    )
```
